32 devices in a mesh: band: 16 (over z, x, core), lev: 2 (over y).
Axes of the slice: x: 2, y: 2, z: 4, core: 2. Of those that a mesh axis runs over, the one named last changes fastest.
Arguments:
- obs_vals: bfloat16 [2, 24, 16384], P('lev', None, 'band'), may hold values from -400 to 400
- obs_colat: bfloat16 [16384], P('band'), may hold values from -1 to 1
- obs_lon: int32 [16384], P('band'), may hold values from 0 to 511
- band_list: int32 [16, 16, 128], P('band'), may hold values from 0 to 1023, as said below
- counts: int32 [16, 16], P('band'), may hold values from 0 to 128, as said below
- w_in: bfloat16 [48, 256], replicated, may hold values from -0.875 to 0.875
- b_in: float32 [256], replicated, may hold values from -3 to 3
- w_out: bfloat16 [256, 256], P(None, 'lev'), may hold values from -0.375 to 0.375
- b_out: float32 [256], P('lev'), may hold values from -3 to 3
Outputs:
- encoded: bfloat16 [256, 512, 128], P('lev', 'band')
The draws below stay inside these ranges and needn't reach their ends.
Inputs may be any that keep to these rules, and one draw needn't show every extreme that they name: For each device s and band b the first counts[s, b] entries of band_list[s, b] are indices (within device s) of observations in band b; over all b they name every observation of device s exactly once. Later entries are padding and name arbitrary observations. `counts`: each row sums to 1024. Some band receives 128 observations from every device.
All inputs are finite; a program needn't handle non-finite values.
Results may differ from the reference program's by a relative error of at most 0.0063.
Values may be sent and summed in bfloat16 or wider, within the bound.
No kernel may reach another device: no remote copies, remote signals or barrier semaphores. Data moves between devices by JAX's collectives and lax.ppermute only.
A program may use at most 64 MiB of HBM per device.

```python
import math
import jax
import jax.numpy as jnp
from jax import lax

CH_OBS = 24
MLP_HID = 256
OUT_CH = 256
LAT_DEV = 8
LON_DEV = 32
CAP = 128
BANDS = 16
LEVELS = 2
FEAT = 48
NLON = 512
OBS_DEV = 1024
OBS_TOTAL = 16384


def draw_obs_vals(key, part):
    base_key = jax.random.fold_in(key, 101)
    key_base, key_chan, key_obs = jax.random.split(base_key, 3)
    full_shape = (LEVELS, CH_OBS, OBS_TOTAL)
    base_vals = jnp.clip(jax.random.normal(key_base, full_shape, jnp.float32), -4.0, 4.0)
    log_top = math.log(10.0)
    chan_scale = jnp.exp(jax.random.uniform(key_chan, (LEVELS, CH_OBS, 1), jnp.float32, 0.0, log_top))
    obs_scale = jnp.exp(jax.random.uniform(key_obs, (1, 1, OBS_TOTAL), jnp.float32, 0.0, log_top))
    return (base_vals * chan_scale * obs_scale).astype(jnp.bfloat16)


def routing(key):
    base_key = jax.random.fold_in(key, 202)
    key_order, key_shift, key_perm = jax.random.split(base_key, 3)
    half_cap = CAP // 2
    band_order = jax.random.permutation(key_order, BANDS)
    count_shift = jax.random.randint(key_shift, (BANDS, BANDS // 2), -half_cap, half_cap + 1)
    count_shift = count_shift.at[:, 0].set(half_cap)
    paired = jnp.stack([half_cap + count_shift, half_cap - count_shift], axis=-1).reshape(BANDS, BANDS)
    counts = jnp.zeros((BANDS, BANDS), jnp.int32).at[:, band_order].set(paired.astype(jnp.int32))
    shuffled = jax.vmap(lambda subkey: jax.random.permutation(subkey, OBS_DEV))(jax.random.split(key_perm, BANDS))
    offsets = jnp.cumsum(counts, axis=1) - counts
    slot_index = (offsets[:, :, None] + jnp.arange(CAP, dtype=jnp.int32)[None, None, :]) % OBS_DEV
    band_list = jax.vmap(lambda perm_row, slot_row: perm_row[slot_row])(shuffled, slot_index)
    return (band_list.astype(jnp.int32), counts)


def draw_band_list(key, part):
    return routing(key)[0]


def draw_counts(key, part):
    return routing(key)[1]


def touch_ends(drawn, rng, least, top_value):
    longest = drawn.shape.index(max(drawn.shape))
    spots = []
    for shift in (0, 1):
        where = [jax.random.randint(jax.random.fold_in(rng, axis), (), 0, length) for axis, length in enumerate(drawn.shape)]
        where[longest] = (where[longest] + shift) % drawn.shape[longest]
        spots.append(tuple(where))
    return drawn.at[spots[0]].set(least).at[spots[1]].set(top_value)


def level_of(own_key, shape, pieces, least, top_value):
    factor_of = 1.0
    for position, shards_of in pieces:
        draws = jax.random.uniform(jax.random.fold_in(jax.random.fold_in(own_key, 6), position), (shards_of,), jnp.float32, least / len(pieces), top_value / len(pieces))
        factor_of = factor_of * jnp.repeat(jnp.exp(draws), shape[position] // shards_of).reshape((-1,) + (1,) * (len(shape) - 1 - position))
    return factor_of


def gaussian(rng, shape, spread, reach, cuts=(), kind=jnp.bfloat16):
    loudness = level_of(rng, shape, cuts, -0.22, 0.18) if cuts else 1.0
    entries = jax.random.normal(rng, shape, jnp.float32) * spread * loudness
    return jnp.minimum(jnp.maximum(entries, -reach), reach).astype(kind)


def setup_inputs(seed: int = 0) -> dict:
    streams_of = jax.random.split(jax.random.key(seed), 10)
    return {
        "obs_vals": draw_obs_vals(jax.random.fold_in(streams_of[9], 71), 0),
        "obs_colat": jnp.clip(jax.random.uniform(streams_of[1], (OBS_TOTAL,), jnp.float32, -1.0, 1.0) * level_of(streams_of[1], (OBS_TOTAL,), ((0, 16),), -0.4, 0.0), -1.0, 1.0).astype(jnp.bfloat16),
        "obs_lon": touch_ends(jax.random.randint(streams_of[2], (OBS_TOTAL,), 0, NLON), jax.random.fold_in(streams_of[2], 1), 0, NLON - 1).astype(jnp.int32),
        "band_list": draw_band_list(jax.random.fold_in(streams_of[9], 71), 0),
        "counts": draw_counts(jax.random.fold_in(streams_of[9], 71), 0),
        "w_in": gaussian(streams_of[5], (FEAT, MLP_HID), FEAT ** -0.5, 0.875),
        "b_in": gaussian(streams_of[6], (MLP_HID,), 0.5, 3.0, (), jnp.float32),
        "w_out": gaussian(streams_of[7], (MLP_HID, OUT_CH), MLP_HID ** -0.5, 0.375, ((1, 2),)),
        "b_out": gaussian(streams_of[8], (OUT_CH,), 0.5, 3.0, ((0, 2),), jnp.float32),
    }


norm_eps = 1e-05

def cheb_inverse(nodes):
    order_ids = jnp.arange(nodes, dtype=jnp.float32)[:, None]
    node_ids = jnp.arange(nodes, dtype=jnp.float32)[None, :]
    factor = jnp.where(order_ids == 0.0, 1.0, 2.0).astype(jnp.float32) / nodes
    return (factor * jnp.cos(math.pi * order_ids * (node_ids + 0.5) / nodes)).astype(jnp.float32)

def lat_weights(colat, nodes):
    angles = jnp.arccos(jnp.clip(colat, -1.0, 1.0))
    order_ids = jnp.arange(nodes, dtype=jnp.float32)
    cheb_terms = jnp.cos(order_ids[:, None] * angles[None, :])
    return jnp.dot(cheb_inverse(nodes).T, cheb_terms, precision=lax.Precision.HIGHEST)

def dct_table(length):
    mode_ids = jnp.arange(length, dtype=jnp.float32)[:, None]
    node_ids = jnp.arange(length, dtype=jnp.float32)[None, :]
    row_scale = jnp.where(mode_ids == 0.0, math.sqrt(1.0 / length), math.sqrt(2.0 / length)).astype(jnp.float32)
    return (row_scale * jnp.cos(math.pi * mode_ids * (node_ids + 0.5) / length)).astype(jnp.bfloat16)

def reference(obs_vals, obs_colat, obs_lon, band_list, counts, w_in, b_in, w_out, b_out):
    lat_count = LAT_DEV * BANDS
    lon_count = LON_DEV * BANDS
    slot_ids = jnp.arange(CAP, dtype=jnp.int32)
    live_slot = slot_ids[None, None, :] < counts[:, :, None]
    source_ids = jnp.arange(BANDS, dtype=jnp.int32)[:, None, None] * OBS_DEV + band_list
    target = jnp.where(live_slot, source_ids, OBS_TOTAL).astype(jnp.int32)
    band_ids = jnp.broadcast_to(jnp.arange(BANDS, dtype=jnp.int32)[None, :, None], target.shape)
    obs_band = jnp.zeros((OBS_TOTAL + 1,), jnp.int32).at[target.reshape(-1)].set(band_ids.reshape(-1))[:OBS_TOTAL]
    weights = lat_weights(obs_colat.astype(jnp.float32), LAT_DEV)
    values = obs_vals.reshape(FEAT, OBS_TOTAL)
    node_ids = jnp.arange(LAT_DEV, dtype=jnp.int32)

    def add_source(grid_sum, source):
        first_obs = (source * OBS_DEV).astype(jnp.int32)
        block_vals = lax.dynamic_slice_in_dim(values, first_obs, OBS_DEV, 1).astype(jnp.float32)
        block_weights = lax.dynamic_slice_in_dim(weights, first_obs, OBS_DEV, 1)
        block_band = lax.dynamic_slice_in_dim(obs_band, first_obs, OBS_DEV, 0)
        block_lon = lax.dynamic_slice_in_dim(obs_lon, first_obs, OBS_DEV, 0)
        weighted = (block_vals[:, None, :] * block_weights[None]).astype(jnp.bfloat16)
        weighted = lax.optimization_barrier(weighted).astype(jnp.float32)
        flat_ids = ((block_band[None, :] * LAT_DEV + node_ids[:, None]) * lon_count + block_lon[None, :]).astype(jnp.int32)
        return (grid_sum.at[:, flat_ids].add(weighted), None)
    grid_sum, _ = lax.scan(add_source, jnp.zeros((FEAT, lat_count * lon_count), jnp.float32), jnp.arange(BANDS, dtype=jnp.int32))
    grid_half = grid_sum.reshape(FEAT, lat_count, lon_count).astype(jnp.bfloat16)
    transform = dct_table(lat_count).astype(jnp.float32)
    spectrum = jnp.einsum('fnm,kn->fmk', grid_half.astype(jnp.float32), transform).astype(jnp.bfloat16)
    blocks = spectrum.reshape(FEAT, BANDS, LON_DEV, lat_count).transpose(1, 0, 2, 3)
    w_first = w_in.astype(jnp.float32)
    w_second = w_out.astype(jnp.float32)

    def encode_block(block):
        feats = block.astype(jnp.float32)
        pre_act = jnp.einsum('fh,fmk->hmk', w_first, feats)
        mean_sq = lax.optimization_barrier(jnp.mean(feats * feats, axis=0))
        hidden = jax.nn.gelu(pre_act * lax.rsqrt(mean_sq + norm_eps)[None] + b_in[:, None, None]).astype(jnp.bfloat16)
        output = jnp.einsum('ho,hmk->omk', w_second, hidden.astype(jnp.float32)) + b_out[:, None, None]
        return output.astype(jnp.bfloat16)
    encoded = lax.map(encode_block, blocks)
    return encoded.transpose(1, 0, 2, 3).reshape(OUT_CH, lon_count, lat_count)
```

```python
import math

import jax
import jax.numpy as jnp
from jax import lax
from jax.experimental import pallas as pl
from jax.experimental.pallas import tpu as pltpu
from jax.sharding import PartitionSpec as P

LAT_DEV = 8
LON_DEV = 32
SUBS = 2
ROWS = 32
LANES = 128

norm_eps = 1e-05
bf16 = jnp.bfloat16
f32 = jnp.float32


def cheb_inverse(nodes):
    order_ids = jnp.arange(nodes, dtype=jnp.float32)[:, None]
    node_ids = jnp.arange(nodes, dtype=jnp.float32)[None, :]
    factor = jnp.where(order_ids == 0.0, 1.0, 2.0).astype(jnp.float32) / nodes
    return factor * jnp.cos(math.pi * order_ids * (node_ids + 0.5) / nodes)


def lat_weights(colat, nodes):
    angles = jnp.arccos(jnp.clip(colat, -1.0, 1.0))
    order_ids = jnp.arange(nodes, dtype=jnp.float32)
    cheb_terms = jnp.cos(order_ids[:, None] * angles[None, :])
    return jnp.dot(cheb_inverse(nodes).T, cheb_terms, precision=lax.Precision.HIGHEST)


def dct_table(length):
    mode_ids = jnp.arange(length, dtype=jnp.float32)[:, None]
    node_ids = jnp.arange(length, dtype=jnp.float32)[None, :]
    row_scale = jnp.where(mode_ids == 0.0, math.sqrt(1.0 / length), math.sqrt(2.0 / length)).astype(
        jnp.float32
    )
    return (row_scale * jnp.cos(math.pi * mode_ids * (node_ids + 0.5) / length)).astype(
        jnp.bfloat16
    )


def by_band(obs_vals, obs_colat, obs_lon, band_list, counts, w_in, b_in, w_out, b_out):
    band_count = lax.axis_size("band")
    capacity = band_list.shape[2]
    lat_nodes = LAT_DEV
    lon_local = LON_DEV
    lon_count = lon_local * band_count
    lat_total = lat_nodes * band_count
    channels = obs_vals.shape[1]
    feat_count = w_in.shape[0]
    picked = band_list[0].reshape(-1)
    live_slot = (jnp.arange(capacity, dtype=jnp.int32)[None, :] < counts[0][:, None]).reshape(-1)
    outgoing = jnp.where(
        live_slot[None, :], jnp.take(obs_vals[0], picked, axis=1), jnp.zeros((), jnp.bfloat16)
    )
    colat_out = jnp.take(obs_colat, picked)[None, :]
    lon_out = jnp.take(obs_lon, picked)[None, :]
    incoming, colat_in, lon_in = (
        lax.all_to_all(outgoing, "band", split_axis=1, concat_axis=1, tiled=True),
        lax.all_to_all(colat_out, "band", split_axis=1, concat_axis=1, tiled=True),
        lax.all_to_all(lon_out, "band", split_axis=1, concat_axis=1, tiled=True),
    )
    weights = lat_weights(colat_in[0].astype(jnp.float32), lat_nodes)
    weighted = (incoming.astype(jnp.float32)[:, None, :] * weights[None]).astype(jnp.bfloat16)
    weighted = weighted.reshape(channels * lat_nodes, -1)
    lon_ids = lon_in[0]
    row_count = weighted.shape[1]
    block_rows = math.gcd(row_count, 1024)
    columns = jnp.arange(lon_count, dtype=jnp.int32)

    def add_block(step_index, grid_sum):
        first_row = step_index * block_rows
        block_vals = lax.dynamic_slice_in_dim(weighted, first_row, block_rows, 1)
        block_lon = lax.dynamic_slice_in_dim(lon_ids, first_row, block_rows, 0)
        onehot = (block_lon[:, None] == columns[None, :]).astype(jnp.bfloat16)
        return grid_sum + jnp.dot(block_vals, onehot, preferred_element_type=jnp.float32)

    grid_sum = lax.fori_loop(
        0,
        row_count // block_rows,
        add_block,
        jnp.zeros((channels * lat_nodes, lon_count), jnp.float32),
    )
    grid_half = grid_sum.astype(jnp.bfloat16).reshape(channels, lat_nodes, lon_count)
    received = lax.all_to_all(grid_half, "band", split_axis=2, concat_axis=2, tiled=True)
    items = received.shape[0]
    arranged = received.reshape(items, lat_nodes, band_count, lon_local)
    table = dct_table(lat_total).reshape(lat_total, band_count, lat_nodes)
    spectrum = jnp.einsum(
        "cjbm,kbj->cmk", arranged, table, preferred_element_type=jnp.float32
    ).astype(jnp.bfloat16)
    shard_rows = lax.all_gather(spectrum, "lev", axis=0, tiled=True)
    pre_act = jnp.einsum("fh,fmk->hmk", w_in, shard_rows, preferred_element_type=jnp.float32)
    squared = shard_rows.astype(jnp.float32)
    pre_act, sum_sq = (pre_act, jnp.sum(squared * squared, axis=0))
    inv_norm = lax.rsqrt(sum_sq * (1.0 / feat_count) + norm_eps)
    hidden = jax.nn.gelu(pre_act * inv_norm[None] + b_in[:, None, None]).astype(jnp.bfloat16)
    output = (
        jnp.einsum("ho,hmk->omk", w_out, hidden, preferred_element_type=jnp.float32)
        + b_out[:, None, None]
    )
    return output.astype(jnp.bfloat16)


def onehot_dot(lhs, rhs, contract):
    return lax.dot_general(lhs, rhs, (contract, ((), ())), preferred_element_type=f32)


def iota(shape, dim):
    return lax.broadcasted_iota(jnp.int32, shape, dim)


def pack_kernel(bands, levels, odd_ref, counts_ref, list_ref, vals_ref, colat_ref, lon_ref, out_ref):
    channels, obs = vals_ref.shape
    blocks = obs // LANES
    low_parts, high_parts = [], []
    for band in range(bands):
        entry = list_ref[band : band + 1, :]
        live = iota((1, LANES), 1) < counts_ref[0, band]
        entry = jnp.where(live, entry, -1)
        high_parts.append(jnp.where((entry >> 7) == iota((blocks, LANES), 0), float(band), 0.0))
        low_parts.append(jnp.where((entry & 127) == iota((LANES, LANES), 0), 1.0, 0.0))
    high = jnp.concatenate(high_parts, axis=1).astype(bf16)
    low = jnp.concatenate(low_parts, axis=1).astype(bf16)
    band_of = onehot_dot(high, low, ((1,), (1,)))
    band_row = jnp.concatenate([band_of[i : i + 1] for i in range(blocks)], axis=1)

    lon = lon_ref[...]
    sub_lons = LON_DEV // SUBS
    cap = LANES // SUBS
    groups = bands * SUBS
    shift = sub_lons.bit_length() - 1
    group = (lon >> shift) ^ odd_ref[0]
    member = jnp.where(group == iota((groups, obs), 0), 1.0, 0.0)
    upper = jnp.where(iota((LANES, LANES), 0) < iota((LANES, LANES), 1), 1.0, 0.0).astype(bf16)
    carry = jnp.zeros((groups, 1), f32)
    places = []
    for i in range(blocks):
        part = member[:, i * LANES : (i + 1) * LANES]
        before = onehot_dot(part.astype(bf16), upper, ((1,), (0,))) + carry
        places.append(jnp.sum(part * before, axis=0, keepdims=True))
        carry = carry + jnp.sum(part, axis=1, keepdims=True)
    place = jnp.concatenate(places, axis=1).astype(jnp.int32)
    overflow = jnp.where(jnp.max(carry) > cap, 1.0, 0.0)
    slot = jnp.where(place < cap, group * cap + place, -1)

    meta = jnp.concatenate(
        [
            (lon & (LON_DEV - 1)).astype(f32),
            band_row,
            colat_ref[...].astype(f32),
            jnp.zeros((ROWS - channels - 3, obs), f32),
        ],
        axis=0,
    )
    table = jnp.concatenate([vals_ref[...].astype(f32), meta], axis=0).astype(bf16)
    flag_row = iota((ROWS, LANES), 0) == channels + 3
    for dest in range(bands):
        onehot = jnp.where(slot == iota((LANES, obs), 0) + dest * LANES, 1.0, 0.0).astype(bf16)
        message = onehot_dot(table, onehot, ((1,), (1,)))
        message = jnp.where(flag_row, overflow, message).astype(bf16)
        for level in range(levels):
            out_ref[level * bands + dest] = message


def cheb_rows(colat):
    nodes = LAT_DEV
    x = jnp.broadcast_to(colat, (nodes, colat.shape[1]))
    node = iota((nodes, 1), 0).astype(f32)
    terms = [jnp.ones_like(x), x]
    for _ in range(nodes - 2):
        terms.append(2.0 * x * terms[-1] - terms[-2])
    total = terms[0] * (1.0 / nodes)
    for order in range(1, nodes):
        scale = jnp.cos((math.pi * order / nodes) * (node + 0.5)) * (2.0 / nodes)
        total = total + terms[order] * scale
    return total


def encode_kernel(
    bands, levels, channels,
    recv_ref, dct_ref, w_in_ref, b_in_ref, w_out_ref, b_out_ref, out_ref,
    spec_ref, turn_ref,
):
    modes = LAT_DEV * bands
    feats = levels * channels
    sub_lons = LON_DEV // SUBS
    slots = bands * (LANES // SUBS)
    lower = iota((ROWS, LANES), 1) < LANES // SUBS

    def half(level, sub):
        pieces = []
        for pair in range(bands // 2):
            even = recv_ref[level * bands + 2 * pair]
            odd = recv_ref[level * bands + 2 * pair + 1]
            pieces.append(jnp.where(lower, even, odd) if sub == 0 else jnp.where(lower, odd, even))
        return jnp.concatenate(pieces, axis=1)

    for sub in range(SUBS):
        parts = [half(level, sub) for level in range(levels)]
        meta = parts[0][channels:].astype(f32)
        values = jnp.concatenate([part[:channels] for part in parts], axis=0)
        lon, band, colat = meta[0:1], meta[1:2], meta[2:3]
        weight = cheb_rows(colat)
        spread = jnp.concatenate(
            [jnp.where(band == float(b), weight, 0.0) for b in range(bands)], axis=0
        ).astype(bf16)
        basis = onehot_dot(dct_ref[...], spread, ((1,), (0,))).astype(bf16)
        for m in range(sub_lons):
            here = jnp.where(lon == float(sub * sub_lons + m), 1.0, 0.0).astype(bf16)
            mine = values * here
            spec_ref[sub * sub_lons + m] = onehot_dot(mine, basis, ((1,), (1,))).astype(bf16)

    w_first = w_in_ref[...].astype(f32).T.astype(bf16)
    w_second = w_out_ref[...].astype(f32).T.astype(bf16)
    b_first = jnp.broadcast_to(b_in_ref[...], (LANES, b_in_ref.shape[1])).T[:, :1]
    b_second = jnp.broadcast_to(b_out_ref[...], (LANES, b_out_ref.shape[1])).T[:, :1]
    out_rows = w_second.shape[0]
    for m in range(LON_DEV):
        spectrum = spec_ref[m]
        wide = spectrum.astype(f32)
        inv_norm = lax.rsqrt(
            jnp.sum(wide * wide, axis=0, keepdims=True) * (1.0 / feats) + norm_eps
        )
        pre_act = onehot_dot(w_first, spectrum, ((1,), (0,)))
        hidden = jax.nn.gelu(pre_act * inv_norm + b_first).astype(bf16)
        encoded = onehot_dot(w_second, hidden, ((1,), (0,))) + b_second
        for i in range(modes // LANES):
            part = encoded[:, i * LANES : (i + 1) * LANES]
            turn_ref[i, pl.ds(m, out_rows, stride=LON_DEV), :] = part
    for i in range(modes // LANES):
        turned = turn_ref[i].reshape(out_rows, LON_DEV, LANES).astype(bf16)
        out_ref[:, :, i * LANES : (i + 1) * LANES] = turned


def on_device(obs_vals, obs_colat, obs_lon, band_list, counts, w_in, b_in, w_out, b_out):
    bands = lax.axis_size("band")
    levels = lax.axis_size("lev")
    channels = obs_vals.shape[1]
    modes = LAT_DEV * bands
    out_rows = w_out.shape[1]
    vmem = pl.BlockSpec(memory_space=pltpu.VMEM)
    smem = pl.BlockSpec(memory_space=pltpu.SMEM)
    odd = (lax.axis_index("band") & 1).astype(jnp.int32).reshape(1)

    packed = pl.pallas_call(
        lambda *refs: pack_kernel(bands, levels, *refs),
        out_shape=jax.ShapeDtypeStruct((levels * bands, ROWS, LANES), bf16),
        in_specs=[smem, smem, vmem, vmem, vmem, vmem],
        out_specs=vmem,
        compiler_params=pltpu.CompilerParams(vmem_limit_bytes=48 << 20),
        name="pack",
    )(odd, counts, band_list[0], obs_vals[0], obs_colat.reshape(1, -1), obs_lon.reshape(1, -1))

    received = lax.all_to_all(packed, ("lev", "band"), split_axis=0, concat_axis=0, tiled=True)
    overflow = jnp.max(received[:, channels + 3, :].astype(f32)) > 0.0

    def by_longitude():
        return pl.pallas_call(
            lambda *refs: encode_kernel(bands, levels, channels, *refs),
            out_shape=jax.ShapeDtypeStruct((out_rows, LON_DEV, modes), bf16),
            in_specs=[vmem] * 6,
            out_specs=vmem,
            scratch_shapes=[
                pltpu.VMEM((LON_DEV, levels * channels, modes), bf16),
                pltpu.VMEM((modes // LANES, out_rows * LON_DEV, LANES), f32),
            ],
            compiler_params=pltpu.CompilerParams(vmem_limit_bytes=48 << 20),
            name="encode",
        )(received, dct_table(modes), w_in, b_in.reshape(1, -1), w_out, b_out.reshape(1, -1))

    def by_bands():
        return by_band(obs_vals, obs_colat, obs_lon, band_list, counts, w_in, b_in, w_out, b_out)

    return lax.cond(overflow, by_bands, by_longitude)


def solution(mesh):
    in_specs = (
        P("lev", None, "band"),
        P("band"),
        P("band"),
        P("band", None, None),
        P("band", None),
        P(),
        P(),
        P(None, "lev"),
        P("lev"),
    )
    out_specs = P("lev", "band", None)
    return jax.shard_map(
        on_device, mesh=mesh, in_specs=in_specs, out_specs=out_specs, check_vma=False
    )
```

```python
import math

import jax
import jax.numpy as jnp
import ml_dtypes
import numpy as np
from jax import lax
from jax.experimental import pallas as pl
from jax.experimental.pallas import tpu as pltpu
from jax.sharding import PartitionSpec as P

LAT_DEV = 8
LON_DEV = 32
SUBS = 2
ROWS = 32
LANES = 128

norm_eps = 1e-05
bf16 = jnp.bfloat16
f32 = jnp.float32


def cheb_inverse(nodes):
    order_ids = jnp.arange(nodes, dtype=jnp.float32)[:, None]
    node_ids = jnp.arange(nodes, dtype=jnp.float32)[None, :]
    factor = jnp.where(order_ids == 0.0, 1.0, 2.0).astype(jnp.float32) / nodes
    return factor * jnp.cos(math.pi * order_ids * (node_ids + 0.5) / nodes)


def lat_weights(colat, nodes):
    angles = jnp.arccos(jnp.clip(colat, -1.0, 1.0))
    order_ids = jnp.arange(nodes, dtype=jnp.float32)
    cheb_terms = jnp.cos(order_ids[:, None] * angles[None, :])
    return jnp.dot(cheb_inverse(nodes).T, cheb_terms, precision=lax.Precision.HIGHEST)


def dct_table(length):
    mode_ids = jnp.arange(length, dtype=jnp.float32)[:, None]
    node_ids = jnp.arange(length, dtype=jnp.float32)[None, :]
    row_scale = jnp.where(mode_ids == 0.0, math.sqrt(1.0 / length), math.sqrt(2.0 / length)).astype(
        jnp.float32
    )
    return (row_scale * jnp.cos(math.pi * mode_ids * (node_ids + 0.5) / length)).astype(
        jnp.bfloat16
    )


def by_band(obs_vals, obs_colat, obs_lon, band_list, counts, w_in, b_in, w_out, b_out):
    band_count = lax.axis_size("band")
    capacity = band_list.shape[2]
    lat_nodes = LAT_DEV
    lon_local = LON_DEV
    lon_count = lon_local * band_count
    lat_total = lat_nodes * band_count
    channels = obs_vals.shape[1]
    feat_count = w_in.shape[0]
    picked = band_list[0].reshape(-1)
    live_slot = (jnp.arange(capacity, dtype=jnp.int32)[None, :] < counts[0][:, None]).reshape(-1)
    outgoing = jnp.where(
        live_slot[None, :], jnp.take(obs_vals[0], picked, axis=1), jnp.zeros((), jnp.bfloat16)
    )
    colat_out = jnp.take(obs_colat, picked)[None, :]
    lon_out = jnp.take(obs_lon, picked)[None, :]
    incoming, colat_in, lon_in = (
        lax.all_to_all(outgoing, "band", split_axis=1, concat_axis=1, tiled=True),
        lax.all_to_all(colat_out, "band", split_axis=1, concat_axis=1, tiled=True),
        lax.all_to_all(lon_out, "band", split_axis=1, concat_axis=1, tiled=True),
    )
    weights = lat_weights(colat_in[0].astype(jnp.float32), lat_nodes)
    weighted = (incoming.astype(jnp.float32)[:, None, :] * weights[None]).astype(jnp.bfloat16)
    weighted = weighted.reshape(channels * lat_nodes, -1)
    lon_ids = lon_in[0]
    row_count = weighted.shape[1]
    block_rows = math.gcd(row_count, 1024)
    columns = jnp.arange(lon_count, dtype=jnp.int32)

    def add_block(step_index, grid_sum):
        first_row = step_index * block_rows
        block_vals = lax.dynamic_slice_in_dim(weighted, first_row, block_rows, 1)
        block_lon = lax.dynamic_slice_in_dim(lon_ids, first_row, block_rows, 0)
        onehot = (block_lon[:, None] == columns[None, :]).astype(jnp.bfloat16)
        return grid_sum + jnp.dot(block_vals, onehot, preferred_element_type=jnp.float32)

    grid_sum = lax.fori_loop(
        0,
        row_count // block_rows,
        add_block,
        jnp.zeros((channels * lat_nodes, lon_count), jnp.float32),
    )
    grid_half = grid_sum.astype(jnp.bfloat16).reshape(channels, lat_nodes, lon_count)
    received = lax.all_to_all(grid_half, "band", split_axis=2, concat_axis=2, tiled=True)
    items = received.shape[0]
    arranged = received.reshape(items, lat_nodes, band_count, lon_local)
    table = dct_table(lat_total).reshape(lat_total, band_count, lat_nodes)
    spectrum = jnp.einsum(
        "cjbm,kbj->cmk", arranged, table, preferred_element_type=jnp.float32
    ).astype(jnp.bfloat16)
    shard_rows = lax.all_gather(spectrum, "lev", axis=0, tiled=True)
    pre_act = jnp.einsum("fh,fmk->hmk", w_in, shard_rows, preferred_element_type=jnp.float32)
    squared = shard_rows.astype(jnp.float32)
    pre_act, sum_sq = (pre_act, jnp.sum(squared * squared, axis=0))
    inv_norm = lax.rsqrt(sum_sq * (1.0 / feat_count) + norm_eps)
    hidden = jax.nn.gelu(pre_act * inv_norm[None] + b_in[:, None, None]).astype(jnp.bfloat16)
    output = (
        jnp.einsum("ho,hmk->omk", w_out, hidden, preferred_element_type=jnp.float32)
        + b_out[:, None, None]
    )
    return output.astype(jnp.bfloat16)


def table_const(length):
    mode_ids = np.arange(length, dtype=np.float32)[:, None]
    node_ids = np.arange(length, dtype=np.float32)[None, :]
    scale = np.where(mode_ids == 0.0, math.sqrt(1.0 / length), math.sqrt(2.0 / length))
    angle = np.float32(math.pi) * mode_ids * (node_ids + np.float32(0.5)) / np.float32(length)
    return (scale.astype(np.float32) * np.cos(angle)).astype(ml_dtypes.bfloat16)


def dot(lhs, rhs, contract):
    return lax.dot_general(lhs, rhs, (contract, ((), ())), preferred_element_type=f32)


def iota(shape, dim):
    return lax.broadcasted_iota(jnp.int32, shape, dim)


def one_where(mask):
    return jnp.where(mask, 1.0, 0.0).astype(bf16)


def row_of(tiles):
    return jnp.concatenate([tiles[i : i + 1] for i in range(tiles.shape[0])], axis=1)


def pack_kernel(bands, levels, odd_ref, counts_ref, list_ref, vals_ref, colat_ref, lon_ref, out_ref):
    channels, obs = vals_ref.shape
    blocks = obs // LANES
    low_parts, high_parts = [], []
    for band in range(bands):
        entry = list_ref[band : band + 1, :]
        entry = jnp.where(iota((1, LANES), 1) < counts_ref[0, band], entry, -1)
        high_parts.append(jnp.where((entry >> 7) == iota((blocks, LANES), 0), float(band), 0.0))
        low_parts.append(one_where((entry & 127) == iota((LANES, LANES), 0)))
    high = jnp.concatenate(high_parts, axis=1).astype(bf16)
    low = jnp.concatenate(low_parts, axis=1)
    band_row = row_of(dot(high, low, ((1,), (1,))))

    lon = row_of(lon_ref[...])
    sub_lons = LON_DEV // SUBS
    cap = LANES // SUBS
    groups = bands * SUBS
    group = (lon // sub_lons) ^ odd_ref[0]
    member = jnp.where(group == iota((groups, obs), 0), 1.0, 0.0)
    earlier = one_where(iota((LANES, LANES), 0) < iota((LANES, LANES), 1))
    carry = jnp.zeros((groups, 1), f32)
    places = []
    for i in range(blocks):
        part = member[:, i * LANES : (i + 1) * LANES]
        before = dot(part.astype(bf16), earlier, ((1,), (0,))) + carry
        places.append(jnp.sum(part * before, axis=0, keepdims=True))
        carry = carry + jnp.sum(part, axis=1, keepdims=True)
    place = jnp.concatenate(places, axis=1).astype(jnp.int32)
    overflow = jnp.where(jnp.max(carry) > cap, 1.0, 0.0)
    slot = jnp.where(place < cap, group * cap + place, -1)

    depth = 2 * LANES
    chunks = obs // depth
    number = iota((1, obs), 1)
    mine = (slot >> 7) == iota((bands, obs), 0)
    held = jnp.where(mine, ((number & (depth - 1)) + 1).astype(f32), 0.0)
    chunk = jnp.where(mine, (number // depth).astype(f32), 0.0)
    lane = one_where((slot & (LANES - 1)) == iota((LANES, obs), 0))
    found = dot(jnp.concatenate([held, chunk], axis=0).astype(bf16), lane, ((1,), (1,)))
    held, chunk = row_of(found[:bands]), row_of(found[bands:])

    rows = jnp.concatenate(
        [
            vals_ref[...].astype(f32),
            (lon & (LON_DEV - 1)).astype(f32),
            band_row,
            row_of(colat_ref[...].astype(f32)),
            jnp.zeros((ROWS - channels - 3, obs), f32),
        ],
        axis=0,
    ).astype(bf16)
    stacked = jnp.concatenate([rows[:, i * depth : (i + 1) * depth] for i in range(chunks)], axis=0)
    pick = one_where(held == (iota((depth, bands * LANES), 0) + 1).astype(f32))
    picked = dot(stacked, pick, ((1,), (0,)))
    messages = jnp.zeros((ROWS, bands * LANES), f32)
    for i in range(chunks):
        messages = jnp.where(chunk == float(i), picked[i * ROWS : (i + 1) * ROWS], messages)
    flag_row = iota((ROWS, LANES), 0) == channels + 3
    for dest in range(bands):
        message = messages[:, dest * LANES : (dest + 1) * LANES]
        message = jnp.where(flag_row, overflow, message).astype(bf16)
        for level in range(levels):
            out_ref[level * bands + dest] = message


def cheb_rows(colat):
    nodes = LAT_DEV
    x = jnp.broadcast_to(colat, (nodes, colat.shape[1]))
    node = iota((nodes, 1), 0).astype(f32)
    twice = x + x
    before, now = jnp.ones_like(x), x
    total = jnp.full_like(x, 1.0 / nodes)
    for order in range(1, nodes):
        scale = jnp.cos((math.pi * order / nodes) * (node + 0.5)) * (2.0 / nodes)
        total = total + now * scale
        before, now = now, twice * now - before
    return total


def gelu(x):
    slope = math.sqrt(2.0 / math.pi)
    half = 0.5 * x
    return half + half * jnp.tanh(x * (slope + (0.044715 * slope) * (x * x)))


def encode_kernel(
    bands, levels, channels,
    recv_ref, dct_ref, w_in_ref, b_in_ref, w_out_ref, b_out_ref, out_ref,
    spread_ref, spec_ref, turn_ref, done_ref, sems,
):
    modes = LAT_DEV * bands
    feats = levels * channels
    sub_lons = LON_DEV // SUBS
    lower = iota((ROWS, LANES), 1) < LANES // SUBS
    w_first = w_in_ref[...].astype(f32).T.astype(bf16)
    w_second = w_out_ref[...].astype(f32).T.astype(bf16)
    out_rows = w_second.shape[0]
    batch = max(1, sub_lons * LANES // modes)
    lane_tiles = batch * modes // LANES
    b_first = jnp.broadcast_to(b_in_ref[...], (LANES, b_in_ref.shape[1])).T
    b_second = jnp.broadcast_to(b_out_ref[...], (LANES, b_out_ref.shape[1])).T
    b_first = jnp.concatenate([b_first] * lane_tiles, axis=1)
    b_second = jnp.concatenate([b_second] * lane_tiles, axis=1)

    def half(level, sub):
        pieces = []
        for pair in range(bands // 2):
            even = recv_ref[level * bands + 2 * pair]
            odd = recv_ref[level * bands + 2 * pair + 1]
            pieces.append(jnp.where(lower, even, odd) if sub == 0 else jnp.where(lower, odd, even))
        return jnp.concatenate(pieces, axis=1)

    for sub in range(SUBS):
        parts = [half(level, sub) for level in range(levels)]
        meta = parts[0][channels:].astype(f32)
        values = jnp.concatenate([part[:channels] for part in parts], axis=0)
        lon, band, colat = meta[0:1], meta[1:2], meta[2:3]
        weight = cheb_rows(colat)
        nodes = jnp.concatenate(
            [jnp.where(band == float(b), weight, 0.0) for b in range(bands)], axis=0
        ).astype(bf16)
        basis = dot(dct_ref[...], nodes, ((1,), (0,))).astype(bf16)
        spread = spread_ref.at[sub % spread_ref.shape[0]]
        for m in range(sub_lons):
            here = one_where(lon == float(sub * sub_lons + m))
            spread[m * feats : (m + 1) * feats, :] = values * here
        spec_ref[sub] = dot(spread[...], basis, ((1,), (1,))).astype(bf16)

    copies = []
    for sub in range(SUBS):
        for first in range(0, sub_lons, batch):
            spectrum = jnp.concatenate(
                [spec_ref[sub, m * feats : (m + 1) * feats, :] for m in range(first, first + batch)],
                axis=1,
            )
            wide = spectrum.astype(f32)
            inv_norm = lax.rsqrt(
                jnp.sum(wide * wide, axis=0, keepdims=True) * (1.0 / feats) + norm_eps
            )
            pre_act = dot(w_first, spectrum, ((1,), (0,)))
            hidden = gelu(pre_act * inv_norm + b_first).astype(bf16)
            encoded = dot(w_second, hidden, ((1,), (0,))) + b_second
            for j in range(batch):
                for i in range(modes // LANES):
                    tile = j * (modes // LANES) + i
                    turn_ref[sub, i, pl.ds(first + j, out_rows, stride=sub_lons), :] = encoded[
                        :, tile * LANES : (tile + 1) * LANES
                    ]
        for i in range(modes // LANES):
            turned = turn_ref[sub, i].reshape(out_rows, sub_lons, LANES).astype(bf16)
            done_ref[sub, :, :, i * LANES : (i + 1) * LANES] = turned
        copy = pltpu.make_async_copy(
            done_ref.at[sub], out_ref.at[:, pl.ds(sub * sub_lons, sub_lons), :], sems.at[sub]
        )
        copy.start()
        copies.append(copy)
    for copy in copies:
        copy.wait()


def on_device(obs_vals, obs_colat, obs_lon, band_list, counts, w_in, b_in, w_out, b_out):
    bands = lax.axis_size("band")
    levels = lax.axis_size("lev")
    channels = obs_vals.shape[1]
    feats = levels * channels
    modes = LAT_DEV * bands
    sub_lons = LON_DEV // SUBS
    slots = bands * LANES // SUBS
    out_rows = w_out.shape[1]
    vmem = pl.BlockSpec(memory_space=pltpu.VMEM)
    smem = pl.BlockSpec(memory_space=pltpu.SMEM)
    odd = (lax.axis_index("band") & 1).astype(jnp.int32).reshape(1)

    packed = pl.pallas_call(
        lambda *refs: pack_kernel(bands, levels, *refs),
        out_shape=pltpu.VMEM((levels * bands, ROWS, LANES), bf16),
        in_specs=[smem, smem, vmem, vmem, vmem, vmem],
        out_specs=vmem,
        compiler_params=pltpu.CompilerParams(vmem_limit_bytes=48 << 20),
        name="pack",
    )(
        odd, counts, band_list[0], obs_vals[0],
        obs_colat.reshape(-1, LANES), obs_lon.reshape(-1, LANES),
    )

    received = lax.all_to_all(packed, ("lev", "band"), split_axis=0, concat_axis=0, tiled=True)
    overflow = jnp.max(received[:, channels + 3, :].astype(f32)) > 0.0

    def by_longitude():
        spread_buffers = SUBS if bands <= 16 else 1
        return pl.pallas_call(
            lambda *refs: encode_kernel(bands, levels, channels, *refs),
            out_shape=jax.ShapeDtypeStruct((out_rows, LON_DEV, modes), bf16),
            in_specs=[vmem] * 6,
            out_specs=pl.BlockSpec(memory_space=pltpu.HBM),
            scratch_shapes=[
                pltpu.VMEM((spread_buffers, sub_lons * feats, slots), bf16),
                pltpu.VMEM((SUBS, sub_lons * feats, modes), bf16),
                pltpu.VMEM((SUBS, modes // LANES, out_rows * sub_lons, LANES), f32),
                pltpu.VMEM((SUBS, out_rows, sub_lons, modes), bf16),
                pltpu.SemaphoreType.DMA((SUBS,)),
            ],
            compiler_params=pltpu.CompilerParams(vmem_limit_bytes=56 << 20),
            name="encode",
        )(received, table_const(modes), w_in, b_in.reshape(1, -1), w_out, b_out.reshape(1, -1))

    def by_bands():
        return by_band(obs_vals, obs_colat, obs_lon, band_list, counts, w_in, b_in, w_out, b_out)

    return lax.cond(overflow, by_bands, by_longitude)


def solution(mesh):
    in_specs = (
        P("lev", None, "band"),
        P("band"),
        P("band"),
        P("band", None, None),
        P("band", None),
        P(),
        P(),
        P(None, "lev"),
        P("lev"),
    )
    out_specs = P("lev", "band", None)
    return jax.shard_map(
        on_device, mesh=mesh, in_specs=in_specs, out_specs=out_specs, check_vma=False
    )
```

```python
import math

import jax
import jax.numpy as jnp
import ml_dtypes
import numpy as np
from jax import lax
from jax.experimental import pallas as pl
from jax.experimental.pallas import tpu as pltpu
from jax.sharding import PartitionSpec as P

LAT_DEV = 8
LON_DEV = 32
SUBS = 2
ROWS = 32
LANES = 128

norm_eps = 1e-05
bf16 = jnp.bfloat16
f32 = jnp.float32


def cheb_inverse(nodes):
    order_ids = jnp.arange(nodes, dtype=jnp.float32)[:, None]
    node_ids = jnp.arange(nodes, dtype=jnp.float32)[None, :]
    factor = jnp.where(order_ids == 0.0, 1.0, 2.0).astype(jnp.float32) / nodes
    return factor * jnp.cos(math.pi * order_ids * (node_ids + 0.5) / nodes)


def lat_weights(colat, nodes):
    angles = jnp.arccos(jnp.clip(colat, -1.0, 1.0))
    order_ids = jnp.arange(nodes, dtype=jnp.float32)
    cheb_terms = jnp.cos(order_ids[:, None] * angles[None, :])
    return jnp.dot(cheb_inverse(nodes).T, cheb_terms, precision=lax.Precision.HIGHEST)


def dct_table(length):
    mode_ids = jnp.arange(length, dtype=jnp.float32)[:, None]
    node_ids = jnp.arange(length, dtype=jnp.float32)[None, :]
    row_scale = jnp.where(mode_ids == 0.0, math.sqrt(1.0 / length), math.sqrt(2.0 / length)).astype(
        jnp.float32
    )
    return (row_scale * jnp.cos(math.pi * mode_ids * (node_ids + 0.5) / length)).astype(
        jnp.bfloat16
    )


def by_band(obs_vals, obs_colat, obs_lon, band_list, counts, w_in, b_in, w_out, b_out):
    band_count = lax.axis_size("band")
    capacity = band_list.shape[2]
    lat_nodes = LAT_DEV
    lon_local = LON_DEV
    lon_count = lon_local * band_count
    lat_total = lat_nodes * band_count
    channels = obs_vals.shape[1]
    feat_count = w_in.shape[0]
    picked = band_list[0].reshape(-1)
    live_slot = (jnp.arange(capacity, dtype=jnp.int32)[None, :] < counts[0][:, None]).reshape(-1)
    outgoing = jnp.where(
        live_slot[None, :], jnp.take(obs_vals[0], picked, axis=1), jnp.zeros((), jnp.bfloat16)
    )
    colat_out = jnp.take(obs_colat, picked)[None, :]
    lon_out = jnp.take(obs_lon, picked)[None, :]
    incoming, colat_in, lon_in = (
        lax.all_to_all(outgoing, "band", split_axis=1, concat_axis=1, tiled=True),
        lax.all_to_all(colat_out, "band", split_axis=1, concat_axis=1, tiled=True),
        lax.all_to_all(lon_out, "band", split_axis=1, concat_axis=1, tiled=True),
    )
    weights = lat_weights(colat_in[0].astype(jnp.float32), lat_nodes)
    weighted = (incoming.astype(jnp.float32)[:, None, :] * weights[None]).astype(jnp.bfloat16)
    weighted = weighted.reshape(channels * lat_nodes, -1)
    lon_ids = lon_in[0]
    row_count = weighted.shape[1]
    block_rows = math.gcd(row_count, 1024)
    columns = jnp.arange(lon_count, dtype=jnp.int32)

    def add_block(step_index, grid_sum):
        first_row = step_index * block_rows
        block_vals = lax.dynamic_slice_in_dim(weighted, first_row, block_rows, 1)
        block_lon = lax.dynamic_slice_in_dim(lon_ids, first_row, block_rows, 0)
        onehot = (block_lon[:, None] == columns[None, :]).astype(jnp.bfloat16)
        return grid_sum + jnp.dot(block_vals, onehot, preferred_element_type=jnp.float32)

    grid_sum = lax.fori_loop(
        0,
        row_count // block_rows,
        add_block,
        jnp.zeros((channels * lat_nodes, lon_count), jnp.float32),
    )
    grid_half = grid_sum.astype(jnp.bfloat16).reshape(channels, lat_nodes, lon_count)
    received = lax.all_to_all(grid_half, "band", split_axis=2, concat_axis=2, tiled=True)
    items = received.shape[0]
    arranged = received.reshape(items, lat_nodes, band_count, lon_local)
    table = dct_table(lat_total).reshape(lat_total, band_count, lat_nodes)
    spectrum = jnp.einsum(
        "cjbm,kbj->cmk", arranged, table, preferred_element_type=jnp.float32
    ).astype(jnp.bfloat16)
    shard_rows = lax.all_gather(spectrum, "lev", axis=0, tiled=True)
    pre_act = jnp.einsum("fh,fmk->hmk", w_in, shard_rows, preferred_element_type=jnp.float32)
    squared = shard_rows.astype(jnp.float32)
    pre_act, sum_sq = (pre_act, jnp.sum(squared * squared, axis=0))
    inv_norm = lax.rsqrt(sum_sq * (1.0 / feat_count) + norm_eps)
    hidden = jax.nn.gelu(pre_act * inv_norm[None] + b_in[:, None, None]).astype(jnp.bfloat16)
    output = (
        jnp.einsum("ho,hmk->omk", w_out, hidden, preferred_element_type=jnp.float32)
        + b_out[:, None, None]
    )
    return output.astype(jnp.bfloat16)


def table_const(length):
    mode_ids = np.arange(length, dtype=np.float32)[:, None]
    node_ids = np.arange(length, dtype=np.float32)[None, :]
    scale = np.where(mode_ids == 0.0, math.sqrt(1.0 / length), math.sqrt(2.0 / length))
    angle = np.float32(math.pi) * mode_ids * (node_ids + np.float32(0.5)) / np.float32(length)
    return (scale.astype(np.float32) * np.cos(angle)).astype(ml_dtypes.bfloat16)


def dot(lhs, rhs, contract):
    return lax.dot_general(lhs, rhs, (contract, ((), ())), preferred_element_type=f32)


def iota(shape, dim):
    return lax.broadcasted_iota(jnp.int32, shape, dim)


def one_where(mask):
    return jnp.where(mask, 1.0, 0.0).astype(bf16)


def row_of(tiles):
    return jnp.concatenate([tiles[i : i + 1] for i in range(tiles.shape[0])], axis=1)


def whole_copy(array):
    def kernel(from_ref, to_ref, sem):
        copy = pltpu.make_async_copy(from_ref, to_ref, sem)
        copy.start()
        copy.wait()

    hbm = pl.BlockSpec(memory_space=pltpu.HBM)
    return pl.pallas_call(
        kernel,
        out_shape=jax.ShapeDtypeStruct(array.shape, array.dtype),
        in_specs=[hbm],
        out_specs=hbm,
        scratch_shapes=[pltpu.SemaphoreType.DMA],
        name="whole_copy",
    )(array)


def pack_kernel(bands, levels, *refs):
    counts_hbm, list_hbm, lon_hbm, colat_hbm, vals_hbm = refs[:5]
    out_ref, counts_ref, list_ref, lon_ref, colat_ref, vals_ref, in_sems = refs[5:]
    loads = [
        pltpu.make_async_copy(source, target, in_sems.at[i])
        for i, (source, target) in enumerate(
            [
                (counts_hbm, counts_ref),
                (list_hbm, list_ref),
                (lon_hbm, lon_ref),
                (colat_hbm, colat_ref),
                (vals_hbm, vals_ref),
            ]
        )
    ]
    for load in loads:
        load.start()
    for load in loads:
        load.wait()
    channels, obs = vals_ref.shape
    blocks = obs // LANES
    low_parts, high_parts = [], []
    for band in range(bands):
        entry = list_ref[band : band + 1, :]
        entry = jnp.where(iota((1, LANES), 1) < counts_ref[0, band], entry, -1)
        high_parts.append(jnp.where((entry >> 7) == iota((blocks, LANES), 0), float(band), 0.0))
        low_parts.append(one_where((entry & 127) == iota((LANES, LANES), 0)))
    high = jnp.concatenate(high_parts, axis=1).astype(bf16)
    low = jnp.concatenate(low_parts, axis=1)
    band_row = row_of(dot(high, low, ((1,), (1,))))

    lon = row_of(lon_ref[...])
    sub_lons = LON_DEV // SUBS
    cap = LANES // SUBS
    groups = bands * SUBS
    odd = lax.axis_index("band") & 1
    group = (lon // sub_lons) ^ odd
    member = jnp.where(group == iota((groups, obs), 0), 1.0, 0.0)
    earlier = one_where(iota((LANES, LANES), 0) < iota((LANES, LANES), 1))
    carry = jnp.zeros((groups, 1), f32)
    places = []
    for i in range(blocks):
        part = member[:, i * LANES : (i + 1) * LANES]
        before = dot(part.astype(bf16), earlier, ((1,), (0,))) + carry
        places.append(jnp.sum(part * before, axis=0, keepdims=True))
        carry = carry + jnp.sum(part, axis=1, keepdims=True)
    place = jnp.concatenate(places, axis=1).astype(jnp.int32)
    overflow = jnp.where(jnp.max(carry) > cap, 1.0, 0.0)
    slot = jnp.where(place < cap, group * cap + place, -1)

    depth = 2 * LANES
    chunks = obs // depth
    number = iota((1, obs), 1)
    mine = (slot >> 7) == iota((bands, obs), 0)
    held = jnp.where(mine, ((number & (depth - 1)) + 1).astype(f32), 0.0)
    chunk = jnp.where(mine, (number // depth).astype(f32), 0.0)
    lane = one_where((slot & (LANES - 1)) == iota((LANES, obs), 0))
    found = dot(jnp.concatenate([held, chunk], axis=0).astype(bf16), lane, ((1,), (1,)))
    held, chunk = row_of(found[:bands]), row_of(found[bands:])

    rows = jnp.concatenate(
        [
            vals_ref[...].astype(f32),
            (lon & (LON_DEV - 1)).astype(f32),
            band_row,
            row_of(colat_ref[...].astype(f32)),
            jnp.zeros((ROWS - channels - 3, obs), f32),
        ],
        axis=0,
    ).astype(bf16)
    stacked = jnp.concatenate([rows[:, i * depth : (i + 1) * depth] for i in range(chunks)], axis=0)
    pick = one_where(held == (iota((depth, bands * LANES), 0) + 1).astype(f32))
    picked = dot(stacked, pick, ((1,), (0,)))
    messages = jnp.zeros((ROWS, bands * LANES), f32)
    for i in range(chunks):
        messages = jnp.where(chunk == float(i), picked[i * ROWS : (i + 1) * ROWS], messages)
    flag_row = iota((ROWS, LANES), 0) == channels + 3
    for dest in range(bands):
        message = messages[:, dest * LANES : (dest + 1) * LANES]
        message = jnp.where(flag_row, overflow, message).astype(bf16)
        for level in range(levels):
            out_ref[level * bands + dest] = message


def cheb_rows(colat):
    nodes = LAT_DEV
    x = jnp.broadcast_to(colat, (nodes, colat.shape[1]))
    node = iota((nodes, 1), 0).astype(f32)
    twice = x + x
    before, now = jnp.ones_like(x), x
    total = jnp.full_like(x, 1.0 / nodes)
    for order in range(1, nodes):
        scale = jnp.cos((math.pi * order / nodes) * (node + 0.5)) * (2.0 / nodes)
        total = total + now * scale
        before, now = now, twice * now - before
    return total


def gelu(x):
    slope = math.sqrt(2.0 / math.pi)
    half = 0.5 * x
    return half + half * jnp.tanh(x * (slope + (0.044715 * slope) * (x * x)))


def encode_kernel(
    bands, levels, channels,
    recv_ref, dct_ref, w_in_ref, b_in_ref, w_out_ref, b_out_ref, out_ref, flag_ref,
    spread_ref, spec_ref, turn_ref, done_ref, mark_ref, sems,
):
    modes = LAT_DEV * bands
    feats = levels * channels
    sub_lons = LON_DEV // SUBS
    lower = iota((ROWS, LANES), 1) < LANES // SUBS
    w_first = w_in_ref[...].astype(f32).T.astype(bf16)
    w_second = w_out_ref[...].astype(f32).T.astype(bf16)
    out_rows = w_second.shape[0]
    batch = max(1, sub_lons * LANES // modes)
    lane_tiles = batch * modes // LANES
    b_first = jnp.broadcast_to(b_in_ref[...], (LANES, b_in_ref.shape[1])).T
    b_second = jnp.broadcast_to(b_out_ref[...], (LANES, b_out_ref.shape[1])).T
    b_first = jnp.concatenate([b_first] * lane_tiles, axis=1)
    b_second = jnp.concatenate([b_second] * lane_tiles, axis=1)

    def half(level, sub):
        pieces = []
        for pair in range(bands // 2):
            even = recv_ref[level * bands + 2 * pair]
            odd = recv_ref[level * bands + 2 * pair + 1]
            pieces.append(jnp.where(lower, even, odd) if sub == 0 else jnp.where(lower, odd, even))
        return jnp.concatenate(pieces, axis=1)

    for sub in range(SUBS):
        parts = [half(level, sub) for level in range(levels)]
        meta = parts[0][channels:].astype(f32)
        values = jnp.concatenate([part[:channels] for part in parts], axis=0)
        lon, band, colat = meta[0:1], meta[1:2], meta[2:3]
        weight = cheb_rows(colat)
        nodes = jnp.concatenate(
            [jnp.where(band == float(b), weight, 0.0) for b in range(bands)], axis=0
        ).astype(bf16)
        basis = dot(dct_ref[...], nodes, ((1,), (0,))).astype(bf16)
        spread = spread_ref.at[sub % spread_ref.shape[0]]
        for m in range(sub_lons):
            here = one_where(lon == float(sub * sub_lons + m))
            spread[m * feats : (m + 1) * feats, :] = values * here
        spec_ref[sub] = dot(spread[...], basis, ((1,), (1,))).astype(bf16)

    flags = recv_ref[0, channels:, :].astype(f32)
    for source in range(1, levels * bands):
        flags = jnp.maximum(flags, recv_ref[source, channels:, :].astype(f32))
    mark_ref[0] = jnp.max(flags[3:4]).astype(jnp.int32)
    copies = [pltpu.make_async_copy(mark_ref, flag_ref, sems.at[SUBS])]
    copies[0].start()
    for sub in range(SUBS):
        for first in range(0, sub_lons, batch):
            spectrum = jnp.concatenate(
                [spec_ref[sub, m * feats : (m + 1) * feats, :] for m in range(first, first + batch)],
                axis=1,
            )
            wide = spectrum.astype(f32)
            inv_norm = lax.rsqrt(
                jnp.sum(wide * wide, axis=0, keepdims=True) * (1.0 / feats) + norm_eps
            )
            pre_act = dot(w_first, spectrum, ((1,), (0,)))
            hidden = gelu(pre_act * inv_norm + b_first).astype(bf16)
            encoded = dot(w_second, hidden, ((1,), (0,))) + b_second
            for j in range(batch):
                for i in range(modes // LANES):
                    tile = j * (modes // LANES) + i
                    turn_ref[sub, i, pl.ds(first + j, out_rows, stride=sub_lons), :] = encoded[
                        :, tile * LANES : (tile + 1) * LANES
                    ]
        for i in range(modes // LANES):
            turned = turn_ref[sub, i].reshape(out_rows, sub_lons, LANES).astype(bf16)
            done_ref[sub, :, :, i * LANES : (i + 1) * LANES] = turned
        copy = pltpu.make_async_copy(
            done_ref.at[sub], out_ref.at[:, pl.ds(sub * sub_lons, sub_lons), :], sems.at[sub]
        )
        copy.start()
        copies.append(copy)
    for copy in copies:
        copy.wait()


def on_device(obs_vals, obs_colat, obs_lon, band_list, counts, w_in, b_in, w_out, b_out):
    bands = lax.axis_size("band")
    levels = lax.axis_size("lev")
    channels = obs_vals.shape[1]
    feats = levels * channels
    modes = LAT_DEV * bands
    sub_lons = LON_DEV // SUBS
    slots = bands * LANES // SUBS
    out_rows = w_out.shape[1]
    vmem = pl.BlockSpec(memory_space=pltpu.VMEM)
    smem = pl.BlockSpec(memory_space=pltpu.SMEM)

    hbm = pl.BlockSpec(memory_space=pltpu.HBM)
    obs = obs_lon.shape[0]
    packed = pl.pallas_call(
        lambda *refs: pack_kernel(bands, levels, *refs),
        out_shape=pltpu.VMEM((levels * bands, ROWS, LANES), bf16),
        in_specs=[hbm] * 5,
        out_specs=vmem,
        scratch_shapes=[
            pltpu.SMEM((1, bands), jnp.int32),
            pltpu.VMEM((bands, LANES), jnp.int32),
            pltpu.VMEM((obs // LANES, LANES), jnp.int32),
            pltpu.VMEM((obs // LANES, LANES), bf16),
            pltpu.VMEM((channels, obs), bf16),
            pltpu.SemaphoreType.DMA((5,)),
        ],
        compiler_params=pltpu.CompilerParams(vmem_limit_bytes=48 << 20),
        name="pack",
    )(
        counts, band_list[0], obs_lon.reshape(-1, LANES), obs_colat.reshape(-1, LANES), obs_vals[0],
    )

    received = lax.all_to_all(packed, ("lev", "band"), split_axis=0, concat_axis=0, tiled=True)
    received = pltpu.with_memory_space_constraint(received, pltpu.VMEM)
    spread_buffers = SUBS if bands <= 16 else 1
    encoded, overflow = pl.pallas_call(
        lambda *refs: encode_kernel(bands, levels, channels, *refs),
        out_shape=[
            jax.ShapeDtypeStruct((out_rows, LON_DEV, modes), bf16),
            jax.ShapeDtypeStruct((1,), jnp.int32),
        ],
        in_specs=[vmem] * 6,
        out_specs=[hbm, hbm],
        scratch_shapes=[
            pltpu.VMEM((spread_buffers, sub_lons * feats, slots), bf16),
            pltpu.VMEM((SUBS, sub_lons * feats, modes), bf16),
            pltpu.VMEM((SUBS, modes // LANES, out_rows * sub_lons, LANES), f32),
            pltpu.VMEM((SUBS, out_rows, sub_lons, modes), bf16),
            pltpu.SMEM((1,), jnp.int32),
            pltpu.SemaphoreType.DMA((SUBS + 1,)),
        ],
        compiler_params=pltpu.CompilerParams(vmem_limit_bytes=56 << 20),
        name="encode",
    )(received, table_const(modes), w_in, b_in.reshape(1, -1), w_out, b_out.reshape(1, -1))

    def by_bands():
        vals = whole_copy(obs_vals)
        return whole_copy(by_band(vals, obs_colat, obs_lon, band_list, counts, w_in, b_in, w_out, b_out))

    def again(carry):
        return by_bands(), jnp.zeros_like(carry[1])

    return lax.while_loop(lambda carry: carry[1][0] > 0, again, (encoded, overflow))[0]


def solution(mesh):
    in_specs = (
        P("lev", None, "band"),
        P("band"),
        P("band"),
        P("band", None, None),
        P("band", None),
        P(),
        P(),
        P(None, "lev"),
        P("lev"),
    )
    out_specs = P("lev", "band", None)
    return jax.shard_map(
        on_device, mesh=mesh, in_specs=in_specs, out_specs=out_specs, check_vma=False
    )
```

```python
import math

import jax
import jax.numpy as jnp
from jax import lax
from jax.experimental import pallas as pl
from jax.experimental.pallas import tpu as pltpu
from jax.sharding import PartitionSpec as P

LAT_DEV = 8
LON_DEV = 32
SUBS = 2
ROWS = 32
LANES = 128

norm_eps = 1e-05
bf16 = jnp.bfloat16
f32 = jnp.float32


def cheb_inverse(nodes):
    order_ids = jnp.arange(nodes, dtype=jnp.float32)[:, None]
    node_ids = jnp.arange(nodes, dtype=jnp.float32)[None, :]
    factor = jnp.where(order_ids == 0.0, 1.0, 2.0).astype(jnp.float32) / nodes
    return factor * jnp.cos(math.pi * order_ids * (node_ids + 0.5) / nodes)


def lat_weights(colat, nodes):
    angles = jnp.arccos(jnp.clip(colat, -1.0, 1.0))
    order_ids = jnp.arange(nodes, dtype=jnp.float32)
    cheb_terms = jnp.cos(order_ids[:, None] * angles[None, :])
    return jnp.dot(cheb_inverse(nodes).T, cheb_terms, precision=lax.Precision.HIGHEST)


def dct_table(length):
    mode_ids = jnp.arange(length, dtype=jnp.float32)[:, None]
    node_ids = jnp.arange(length, dtype=jnp.float32)[None, :]
    row_scale = jnp.where(mode_ids == 0.0, math.sqrt(1.0 / length), math.sqrt(2.0 / length)).astype(
        jnp.float32
    )
    return (row_scale * jnp.cos(math.pi * mode_ids * (node_ids + 0.5) / length)).astype(
        jnp.bfloat16
    )


def by_band(obs_vals, obs_colat, obs_lon, band_list, counts, w_in, b_in, w_out, b_out):
    band_count = lax.axis_size("band")
    capacity = band_list.shape[2]
    lat_nodes = LAT_DEV
    lon_local = LON_DEV
    lon_count = lon_local * band_count
    lat_total = lat_nodes * band_count
    channels = obs_vals.shape[1]
    feat_count = w_in.shape[0]
    picked = band_list[0].reshape(-1)
    live_slot = (jnp.arange(capacity, dtype=jnp.int32)[None, :] < counts[0][:, None]).reshape(-1)
    outgoing = jnp.where(
        live_slot[None, :], jnp.take(obs_vals[0], picked, axis=1), jnp.zeros((), jnp.bfloat16)
    )
    colat_out = jnp.take(obs_colat, picked)[None, :]
    lon_out = jnp.take(obs_lon, picked)[None, :]
    incoming, colat_in, lon_in = (
        lax.all_to_all(outgoing, "band", split_axis=1, concat_axis=1, tiled=True),
        lax.all_to_all(colat_out, "band", split_axis=1, concat_axis=1, tiled=True),
        lax.all_to_all(lon_out, "band", split_axis=1, concat_axis=1, tiled=True),
    )
    weights = lat_weights(colat_in[0].astype(jnp.float32), lat_nodes)
    weighted = (incoming.astype(jnp.float32)[:, None, :] * weights[None]).astype(jnp.bfloat16)
    weighted = weighted.reshape(channels * lat_nodes, -1)
    lon_ids = lon_in[0]
    row_count = weighted.shape[1]
    block_rows = math.gcd(row_count, 1024)
    columns = jnp.arange(lon_count, dtype=jnp.int32)

    def add_block(step_index, grid_sum):
        first_row = step_index * block_rows
        block_vals = lax.dynamic_slice_in_dim(weighted, first_row, block_rows, 1)
        block_lon = lax.dynamic_slice_in_dim(lon_ids, first_row, block_rows, 0)
        onehot = (block_lon[:, None] == columns[None, :]).astype(jnp.bfloat16)
        return grid_sum + jnp.dot(block_vals, onehot, preferred_element_type=jnp.float32)

    grid_sum = lax.fori_loop(
        0,
        row_count // block_rows,
        add_block,
        jnp.zeros((channels * lat_nodes, lon_count), jnp.float32),
    )
    grid_half = grid_sum.astype(jnp.bfloat16).reshape(channels, lat_nodes, lon_count)
    received = lax.all_to_all(grid_half, "band", split_axis=2, concat_axis=2, tiled=True)
    items = received.shape[0]
    arranged = received.reshape(items, lat_nodes, band_count, lon_local)
    table = dct_table(lat_total).reshape(lat_total, band_count, lat_nodes)
    spectrum = jnp.einsum(
        "cjbm,kbj->cmk", arranged, table, preferred_element_type=jnp.float32
    ).astype(jnp.bfloat16)
    shard_rows = lax.all_gather(spectrum, "lev", axis=0, tiled=True)
    pre_act = jnp.einsum("fh,fmk->hmk", w_in, shard_rows, preferred_element_type=jnp.float32)
    squared = shard_rows.astype(jnp.float32)
    pre_act, sum_sq = (pre_act, jnp.sum(squared * squared, axis=0))
    inv_norm = lax.rsqrt(sum_sq * (1.0 / feat_count) + norm_eps)
    hidden = jax.nn.gelu(pre_act * inv_norm[None] + b_in[:, None, None]).astype(jnp.bfloat16)
    output = (
        jnp.einsum("ho,hmk->omk", w_out, hidden, preferred_element_type=jnp.float32)
        + b_out[:, None, None]
    )
    return output.astype(jnp.bfloat16)


def dot(lhs, rhs, contract):
    return lax.dot_general(lhs, rhs, (contract, ((), ())), preferred_element_type=f32)


def iota(shape, dim):
    return lax.broadcasted_iota(jnp.int32, shape, dim)


def one_where(mask):
    return jnp.where(mask, 1.0, 0.0).astype(bf16)


def cosine_rows(length):
    mode = iota((length, length), 0)
    angle = (mode * (2 * iota((length, length), 1) + 1)) & (4 * length - 1)
    scale = jnp.where(mode == 0, math.sqrt(1.0 / length), math.sqrt(2.0 / length))
    return (scale * jnp.cos(angle.astype(f32) * (math.pi / (2 * length)))).astype(bf16)


def row_of(tiles):
    return jnp.concatenate([tiles[i : i + 1] for i in range(tiles.shape[0])], axis=1)


def whole_copy(array):
    def kernel(from_ref, to_ref, sem):
        copy = pltpu.make_async_copy(from_ref, to_ref, sem)
        copy.start()
        copy.wait()

    hbm = pl.BlockSpec(memory_space=pltpu.HBM)
    return pl.pallas_call(
        kernel,
        out_shape=jax.ShapeDtypeStruct(array.shape, array.dtype),
        in_specs=[hbm],
        out_specs=hbm,
        scratch_shapes=[pltpu.SemaphoreType.DMA],
        name="whole_copy",
    )(array)


def pack_kernel(bands, levels, *refs):
    counts_hbm, list_hbm, lon_hbm, colat_hbm, vals_hbm = refs[:5]
    layers_hbm, out_ref, layers_ref, dct_ref = refs[5:9], refs[9], refs[10:14], refs[14]
    counts_ref, list_ref, lon_ref, colat_ref, vals_ref, in_sems, layer_sems = refs[15:]
    loads = [
        pltpu.make_async_copy(source, target, in_sems.at[i])
        for i, (source, target) in enumerate(
            [
                (counts_hbm, counts_ref),
                (list_hbm, list_ref),
                (lon_hbm, lon_ref),
                (colat_hbm, colat_ref),
                (vals_hbm, vals_ref),
            ]
        )
    ]
    layers = [
        pltpu.make_async_copy(source, target, layer_sems.at[i])
        for i, (source, target) in enumerate(zip(layers_hbm, layers_ref))
    ]
    for load in loads + layers:
        load.start()
    dct_ref[...] = cosine_rows(dct_ref.shape[0])
    for load in loads:
        load.wait()
    channels, obs = vals_ref.shape
    blocks = obs // LANES
    low_parts, high_parts = [], []
    for band in range(bands):
        entry = list_ref[band : band + 1, :]
        entry = jnp.where(iota((1, LANES), 1) < counts_ref[0, band], entry, -1)
        high_parts.append(jnp.where((entry >> 7) == iota((blocks, LANES), 0), float(band), 0.0))
        low_parts.append(one_where((entry & 127) == iota((LANES, LANES), 0)))
    high = jnp.concatenate(high_parts, axis=1).astype(bf16)
    low = jnp.concatenate(low_parts, axis=1)
    band_row = row_of(dot(high, low, ((1,), (1,))))

    lon = row_of(lon_ref[...])
    sub_lons = LON_DEV // SUBS
    cap = LANES // SUBS
    groups = bands * SUBS
    odd = lax.axis_index("band") & 1
    group = (lon // sub_lons) ^ odd
    member = jnp.where(group == iota((groups, obs), 0), 1.0, 0.0)
    earlier = one_where(iota((LANES, LANES), 0) < iota((LANES, LANES), 1))
    carry = jnp.zeros((groups, 1), f32)
    places = []
    for i in range(blocks):
        part = member[:, i * LANES : (i + 1) * LANES]
        before = dot(part.astype(bf16), earlier, ((1,), (0,))) + carry
        places.append(jnp.sum(part * before, axis=0, keepdims=True))
        carry = carry + jnp.sum(part, axis=1, keepdims=True)
    place = jnp.concatenate(places, axis=1).astype(jnp.int32)
    overflow = jnp.where(jnp.max(carry) > cap, 1.0, 0.0)
    slot = jnp.where(place < cap, group * cap + place, -1)

    depth = 2 * LANES
    chunks = obs // depth
    number = iota((1, obs), 1)
    mine = (slot >> 7) == iota((bands, obs), 0)
    held = jnp.where(mine, ((number & (depth - 1)) + 1).astype(f32), 0.0)
    chunk = jnp.where(mine, (number // depth).astype(f32), 0.0)
    lane = one_where((slot & (LANES - 1)) == iota((LANES, obs), 0))
    found = dot(jnp.concatenate([held, chunk], axis=0).astype(bf16), lane, ((1,), (1,)))
    held, chunk = row_of(found[:bands]), row_of(found[bands:])

    rows = jnp.concatenate(
        [
            vals_ref[...].astype(f32),
            (lon & (LON_DEV - 1)).astype(f32),
            band_row,
            row_of(colat_ref[...].astype(f32)),
            jnp.zeros((ROWS - channels - 3, obs), f32),
        ],
        axis=0,
    ).astype(bf16)
    stacked = jnp.concatenate([rows[:, i * depth : (i + 1) * depth] for i in range(chunks)], axis=0)
    pick = one_where(held == (iota((depth, bands * LANES), 0) + 1).astype(f32))
    picked = dot(stacked, pick, ((1,), (0,)))
    messages = jnp.zeros((ROWS, bands * LANES), f32)
    for i in range(chunks):
        messages = jnp.where(chunk == float(i), picked[i * ROWS : (i + 1) * ROWS], messages)
    flag_row = iota((ROWS, LANES), 0) == channels + 3
    for dest in range(bands):
        message = messages[:, dest * LANES : (dest + 1) * LANES]
        message = jnp.where(flag_row, overflow, message).astype(bf16)
        for level in range(levels):
            out_ref[level * bands + dest] = message
    for layer in layers:
        layer.wait()


def cheb_rows(colat):
    nodes = LAT_DEV
    x = jnp.broadcast_to(colat, (nodes, colat.shape[1]))
    node = iota((nodes, 1), 0).astype(f32)
    twice = x + x
    before, now = jnp.ones_like(x), x
    total = jnp.full_like(x, 1.0 / nodes)
    for order in range(1, nodes):
        scale = jnp.cos((math.pi * order / nodes) * (node + 0.5)) * (2.0 / nodes)
        total = total + now * scale
        before, now = now, twice * now - before
    return total


def gelu(x):
    slope = math.sqrt(2.0 / math.pi)
    half = 0.5 * x
    return half + half * jnp.tanh(x * (slope + (0.044715 * slope) * (x * x)))


def encode_kernel(
    bands, levels, channels,
    recv_ref, w_in_ref, b_in_ref, w_out_ref, b_out_ref, dct_ref, out_ref, flag_ref,
    spread_ref, spec_ref, turn_ref, done_ref, mark_ref, sems,
):
    modes = LAT_DEV * bands
    feats = levels * channels
    sub_lons = LON_DEV // SUBS
    lower = iota((ROWS, LANES), 1) < LANES // SUBS
    w_first = w_in_ref[...].astype(f32).T.astype(bf16)
    w_second = w_out_ref[...].astype(f32).T.astype(bf16)
    out_rows = w_second.shape[0]
    batch = max(1, sub_lons * LANES // modes)
    lane_tiles = batch * modes // LANES
    b_first = jnp.broadcast_to(b_in_ref[...], (LANES, b_in_ref.shape[1])).T
    b_second = jnp.broadcast_to(b_out_ref[...], (LANES, b_out_ref.shape[1])).T
    b_first = jnp.concatenate([b_first] * lane_tiles, axis=1)
    b_second = jnp.concatenate([b_second] * lane_tiles, axis=1)

    def half(level, sub):
        pieces = []
        for pair in range(bands // 2):
            even = recv_ref[level * bands + 2 * pair]
            odd = recv_ref[level * bands + 2 * pair + 1]
            pieces.append(jnp.where(lower, even, odd) if sub == 0 else jnp.where(lower, odd, even))
        return jnp.concatenate(pieces, axis=1)

    for sub in range(SUBS):
        parts = [half(level, sub) for level in range(levels)]
        meta = parts[0][channels:].astype(f32)
        values = jnp.concatenate([part[:channels] for part in parts], axis=0)
        lon, band, colat = meta[0:1], meta[1:2], meta[2:3]
        weight = cheb_rows(colat)
        nodes = jnp.concatenate(
            [jnp.where(band == float(b), weight, 0.0) for b in range(bands)], axis=0
        ).astype(bf16)
        basis = dot(dct_ref[...], nodes, ((1,), (0,))).astype(bf16)
        spread = spread_ref.at[sub % spread_ref.shape[0]]
        for m in range(sub_lons):
            here = one_where(lon == float(sub * sub_lons + m))
            spread[m * feats : (m + 1) * feats, :] = values * here
        spec_ref[sub] = dot(spread[...], basis, ((1,), (1,))).astype(bf16)

    flags = recv_ref[0, channels:, :].astype(f32)
    for source in range(1, levels * bands):
        flags = jnp.maximum(flags, recv_ref[source, channels:, :].astype(f32))
    mark_ref[0] = jnp.max(flags[3:4]).astype(jnp.int32)
    copies = [pltpu.make_async_copy(mark_ref, flag_ref, sems.at[SUBS])]
    copies[0].start()
    for sub in range(SUBS):
        for first in range(0, sub_lons, batch):
            spectrum = jnp.concatenate(
                [spec_ref[sub, m * feats : (m + 1) * feats, :] for m in range(first, first + batch)],
                axis=1,
            )
            wide = spectrum.astype(f32)
            inv_norm = lax.rsqrt(
                jnp.sum(wide * wide, axis=0, keepdims=True) * (1.0 / feats) + norm_eps
            )
            pre_act = dot(w_first, spectrum, ((1,), (0,)))
            hidden = gelu(pre_act * inv_norm + b_first).astype(bf16)
            encoded = dot(w_second, hidden, ((1,), (0,))) + b_second
            for j in range(batch):
                for i in range(modes // LANES):
                    tile = j * (modes // LANES) + i
                    turn_ref[sub, i, pl.ds(first + j, out_rows, stride=sub_lons), :] = encoded[
                        :, tile * LANES : (tile + 1) * LANES
                    ]
        for i in range(modes // LANES):
            turned = turn_ref[sub, i].reshape(out_rows, sub_lons, LANES).astype(bf16)
            done_ref[sub, :, :, i * LANES : (i + 1) * LANES] = turned
        copy = pltpu.make_async_copy(
            done_ref.at[sub], out_ref.at[:, pl.ds(sub * sub_lons, sub_lons), :], sems.at[sub]
        )
        copy.start()
        copies.append(copy)
    for copy in copies:
        copy.wait()


def on_device(obs_vals, obs_colat, obs_lon, band_list, counts, w_in, b_in, w_out, b_out):
    bands = lax.axis_size("band")
    levels = lax.axis_size("lev")
    channels = obs_vals.shape[1]
    feats = levels * channels
    modes = LAT_DEV * bands
    sub_lons = LON_DEV // SUBS
    slots = bands * LANES // SUBS
    out_rows = w_out.shape[1]
    vmem = pl.BlockSpec(memory_space=pltpu.VMEM)
    smem = pl.BlockSpec(memory_space=pltpu.SMEM)

    hbm = pl.BlockSpec(memory_space=pltpu.HBM)
    obs = obs_lon.shape[0]
    layers = [w_in, b_in.reshape(1, -1), w_out, b_out.reshape(1, -1)]
    packed, *layers = pl.pallas_call(
        lambda *refs: pack_kernel(bands, levels, *refs),
        out_shape=[pltpu.VMEM((levels * bands, ROWS, LANES), bf16)]
        + [pltpu.VMEM(layer.shape, layer.dtype) for layer in layers]
        + [pltpu.VMEM((modes, modes), bf16)],
        in_specs=[hbm] * 9,
        out_specs=[vmem] * 6,
        scratch_shapes=[
            pltpu.SMEM((1, bands), jnp.int32),
            pltpu.VMEM((bands, LANES), jnp.int32),
            pltpu.VMEM((obs // LANES, LANES), jnp.int32),
            pltpu.VMEM((obs // LANES, LANES), bf16),
            pltpu.VMEM((channels, obs), bf16),
            pltpu.SemaphoreType.DMA((5,)),
            pltpu.SemaphoreType.DMA((4,)),
        ],
        compiler_params=pltpu.CompilerParams(vmem_limit_bytes=(16 if bands <= 16 else 48) << 20),
        name="pack",
    )(
        counts, band_list[0], obs_lon.reshape(-1, LANES), obs_colat.reshape(-1, LANES), obs_vals[0],
        *layers,
    )

    received = lax.all_to_all(packed, ("lev", "band"), split_axis=0, concat_axis=0, tiled=True)
    received = pltpu.with_memory_space_constraint(received, pltpu.VMEM)
    spread_buffers = SUBS if bands <= 16 else 1
    encoded, overflow = pl.pallas_call(
        lambda *refs: encode_kernel(bands, levels, channels, *refs),
        out_shape=[
            jax.ShapeDtypeStruct((out_rows, LON_DEV, modes), bf16),
            jax.ShapeDtypeStruct((1,), jnp.int32),
        ],
        in_specs=[vmem] * 6,
        out_specs=[hbm, hbm],
        scratch_shapes=[
            pltpu.VMEM((spread_buffers, sub_lons * feats, slots), bf16),
            pltpu.VMEM((SUBS, sub_lons * feats, modes), bf16),
            pltpu.VMEM((SUBS, modes // LANES, out_rows * sub_lons, LANES), f32),
            pltpu.VMEM((SUBS, out_rows, sub_lons, modes), bf16),
            pltpu.SMEM((1,), jnp.int32),
            pltpu.SemaphoreType.DMA((SUBS + 1,)),
        ],
        compiler_params=pltpu.CompilerParams(vmem_limit_bytes=(24 if bands <= 16 else 56) << 20),
        name="encode",
    )(received, *layers)

    def by_bands():
        vals = whole_copy(obs_vals)
        return whole_copy(by_band(vals, obs_colat, obs_lon, band_list, counts, w_in, b_in, w_out, b_out))

    def again(carry):
        return by_bands(), jnp.zeros_like(carry[1])

    return lax.while_loop(lambda carry: carry[1][0] > 0, again, (encoded, overflow))[0]


def solution(mesh):
    in_specs = (
        P("lev", None, "band"),
        P("band"),
        P("band"),
        P("band", None, None),
        P("band", None),
        P(),
        P(),
        P(None, "lev"),
        P("lev"),
    )
    out_specs = P("lev", "band", None)
    return jax.shard_map(
        on_device, mesh=mesh, in_specs=in_specs, out_specs=out_specs, check_vma=False
    )
```

```python
import math

import jax
import jax.numpy as jnp
from jax import lax
from jax.experimental import pallas as pl
from jax.experimental.pallas import tpu as pltpu
from jax.sharding import PartitionSpec as P

LAT_DEV = 8
LON_DEV = 32
SUBS = 2
ROWS = 32
LANES = 128

norm_eps = 1e-05
bf16 = jnp.bfloat16
f32 = jnp.float32


def cheb_inverse(nodes):
    order_ids = jnp.arange(nodes, dtype=jnp.float32)[:, None]
    node_ids = jnp.arange(nodes, dtype=jnp.float32)[None, :]
    factor = jnp.where(order_ids == 0.0, 1.0, 2.0).astype(jnp.float32) / nodes
    return factor * jnp.cos(math.pi * order_ids * (node_ids + 0.5) / nodes)


def lat_weights(colat, nodes):
    angles = jnp.arccos(jnp.clip(colat, -1.0, 1.0))
    order_ids = jnp.arange(nodes, dtype=jnp.float32)
    cheb_terms = jnp.cos(order_ids[:, None] * angles[None, :])
    return jnp.dot(cheb_inverse(nodes).T, cheb_terms, precision=lax.Precision.HIGHEST)


def dct_table(length):
    mode_ids = jnp.arange(length, dtype=jnp.float32)[:, None]
    node_ids = jnp.arange(length, dtype=jnp.float32)[None, :]
    row_scale = jnp.where(mode_ids == 0.0, math.sqrt(1.0 / length), math.sqrt(2.0 / length)).astype(
        jnp.float32
    )
    return (row_scale * jnp.cos(math.pi * mode_ids * (node_ids + 0.5) / length)).astype(
        jnp.bfloat16
    )


def by_band(obs_vals, obs_colat, obs_lon, band_list, counts, w_in, b_in, w_out, b_out):
    band_count = lax.axis_size("band")
    capacity = band_list.shape[2]
    lat_nodes = LAT_DEV
    lon_local = LON_DEV
    lon_count = lon_local * band_count
    lat_total = lat_nodes * band_count
    channels = obs_vals.shape[1]
    feat_count = w_in.shape[0]
    picked = band_list[0].reshape(-1)
    live_slot = (jnp.arange(capacity, dtype=jnp.int32)[None, :] < counts[0][:, None]).reshape(-1)
    outgoing = jnp.where(
        live_slot[None, :], jnp.take(obs_vals[0], picked, axis=1), jnp.zeros((), jnp.bfloat16)
    )
    colat_out = jnp.take(obs_colat, picked)[None, :]
    lon_out = jnp.take(obs_lon, picked)[None, :]
    incoming, colat_in, lon_in = (
        lax.all_to_all(outgoing, "band", split_axis=1, concat_axis=1, tiled=True),
        lax.all_to_all(colat_out, "band", split_axis=1, concat_axis=1, tiled=True),
        lax.all_to_all(lon_out, "band", split_axis=1, concat_axis=1, tiled=True),
    )
    weights = lat_weights(colat_in[0].astype(jnp.float32), lat_nodes)
    weighted = (incoming.astype(jnp.float32)[:, None, :] * weights[None]).astype(jnp.bfloat16)
    weighted = weighted.reshape(channels * lat_nodes, -1)
    lon_ids = lon_in[0]
    row_count = weighted.shape[1]
    block_rows = math.gcd(row_count, 1024)
    columns = jnp.arange(lon_count, dtype=jnp.int32)

    def add_block(step_index, grid_sum):
        first_row = step_index * block_rows
        block_vals = lax.dynamic_slice_in_dim(weighted, first_row, block_rows, 1)
        block_lon = lax.dynamic_slice_in_dim(lon_ids, first_row, block_rows, 0)
        onehot = (block_lon[:, None] == columns[None, :]).astype(jnp.bfloat16)
        return grid_sum + jnp.dot(block_vals, onehot, preferred_element_type=jnp.float32)

    grid_sum = lax.fori_loop(
        0,
        row_count // block_rows,
        add_block,
        jnp.zeros((channels * lat_nodes, lon_count), jnp.float32),
    )
    grid_half = grid_sum.astype(jnp.bfloat16).reshape(channels, lat_nodes, lon_count)
    received = lax.all_to_all(grid_half, "band", split_axis=2, concat_axis=2, tiled=True)
    items = received.shape[0]
    arranged = received.reshape(items, lat_nodes, band_count, lon_local)
    table = dct_table(lat_total).reshape(lat_total, band_count, lat_nodes)
    spectrum = jnp.einsum(
        "cjbm,kbj->cmk", arranged, table, preferred_element_type=jnp.float32
    ).astype(jnp.bfloat16)
    shard_rows = lax.all_gather(spectrum, "lev", axis=0, tiled=True)
    pre_act = jnp.einsum("fh,fmk->hmk", w_in, shard_rows, preferred_element_type=jnp.float32)
    squared = shard_rows.astype(jnp.float32)
    pre_act, sum_sq = (pre_act, jnp.sum(squared * squared, axis=0))
    inv_norm = lax.rsqrt(sum_sq * (1.0 / feat_count) + norm_eps)
    hidden = jax.nn.gelu(pre_act * inv_norm[None] + b_in[:, None, None]).astype(jnp.bfloat16)
    output = (
        jnp.einsum("ho,hmk->omk", w_out, hidden, preferred_element_type=jnp.float32)
        + b_out[:, None, None]
    )
    return output.astype(jnp.bfloat16)


def dot(lhs, rhs, contract):
    return lax.dot_general(lhs, rhs, (contract, ((), ())), preferred_element_type=f32)


def iota(shape, dim):
    return lax.broadcasted_iota(jnp.int32, shape, dim)


def one_where(mask):
    return jnp.where(mask, 1.0, 0.0).astype(bf16)


def cosine_rows(length):
    mode = iota((length, length), 0)
    angle = (mode * (2 * iota((length, length), 1) + 1)) & (4 * length - 1)
    scale = jnp.where(mode == 0, math.sqrt(1.0 / length), math.sqrt(2.0 / length))
    return (scale * jnp.cos(angle.astype(f32) * (math.pi / (2 * length)))).astype(bf16)


def row_of(tiles):
    return jnp.concatenate([tiles[i : i + 1] for i in range(tiles.shape[0])], axis=1)


def whole_copy(array):
    def kernel(from_ref, to_ref, sem):
        copy = pltpu.make_async_copy(from_ref, to_ref, sem)
        copy.start()
        copy.wait()

    hbm = pl.BlockSpec(memory_space=pltpu.HBM)
    return pl.pallas_call(
        kernel,
        out_shape=jax.ShapeDtypeStruct(array.shape, array.dtype),
        in_specs=[hbm],
        out_specs=hbm,
        scratch_shapes=[pltpu.SemaphoreType.DMA],
        name="whole_copy",
    )(array)


def pack_kernel(bands, levels, *refs):
    counts_hbm, list_hbm, lon_hbm, colat_hbm, vals_hbm = refs[:5]
    layers_hbm, out_ref, layers_ref, dct_ref = refs[5:9], refs[9], refs[10:14], refs[14]
    counts_ref, list_ref, lon_ref, colat_ref, vals_ref, in_sems, layer_sems = refs[15:]
    loads = [
        pltpu.make_async_copy(source, target, in_sems.at[i])
        for i, (source, target) in enumerate(
            [
                (counts_hbm, counts_ref),
                (list_hbm, list_ref),
                (lon_hbm, lon_ref),
                (colat_hbm, colat_ref),
                (vals_hbm, vals_ref),
            ]
        )
    ]
    layers = [
        pltpu.make_async_copy(source, target, layer_sems.at[i])
        for i, (source, target) in enumerate(zip(layers_hbm, layers_ref))
    ]
    for load in loads + layers:
        load.start()
    dct_ref[...] = cosine_rows(dct_ref.shape[0])
    for load in loads:
        load.wait()
    channels, obs = vals_ref.shape
    blocks = obs // LANES
    low_parts, high_parts = [], []
    for band in range(bands):
        entry = list_ref[band : band + 1, :]
        entry = jnp.where(iota((1, LANES), 1) < counts_ref[0, band], entry, -1)
        high_parts.append(jnp.where((entry >> 7) == iota((blocks, LANES), 0), float(band), 0.0))
        low_parts.append(one_where((entry & 127) == iota((LANES, LANES), 0)))
    high = jnp.concatenate(high_parts, axis=1).astype(bf16)
    low = jnp.concatenate(low_parts, axis=1)
    band_row = row_of(dot(high, low, ((1,), (1,))))

    lon = row_of(lon_ref[...])
    sub_lons = LON_DEV // SUBS
    cap = LANES // SUBS
    groups = bands * SUBS
    odd = lax.axis_index("band") & 1
    group = (lon // sub_lons) ^ odd
    member = jnp.where(group == iota((groups, obs), 0), 1.0, 0.0)
    earlier = one_where(iota((LANES, LANES), 0) < iota((LANES, LANES), 1))
    carry = jnp.zeros((groups, 1), f32)
    places = []
    for i in range(blocks):
        part = member[:, i * LANES : (i + 1) * LANES]
        before = dot(part.astype(bf16), earlier, ((1,), (0,))) + carry
        places.append(jnp.sum(part * before, axis=0, keepdims=True))
        carry = carry + jnp.sum(part, axis=1, keepdims=True)
    place = jnp.concatenate(places, axis=1).astype(jnp.int32)
    overflow = jnp.where(jnp.max(carry) > cap, 1.0, 0.0)
    slot = jnp.where(place < cap, group * cap + place, -1)

    depth = 2 * LANES
    chunks = obs // depth
    number = iota((1, obs), 1)
    mine = (slot >> 7) == iota((bands, obs), 0)
    held = jnp.where(mine, ((number & (depth - 1)) + 1).astype(f32), 0.0)
    chunk = jnp.where(mine, (number // depth).astype(f32), 0.0)
    lane = one_where((slot & (LANES - 1)) == iota((LANES, obs), 0))
    found = dot(jnp.concatenate([held, chunk], axis=0).astype(bf16), lane, ((1,), (1,)))
    held, chunk = row_of(found[:bands]), row_of(found[bands:])

    rows = jnp.concatenate(
        [
            vals_ref[...].astype(f32),
            (lon & (LON_DEV - 1)).astype(f32),
            band_row,
            row_of(colat_ref[...].astype(f32)),
            jnp.zeros((ROWS - channels - 3, obs), f32),
        ],
        axis=0,
    ).astype(bf16)
    stacked = jnp.concatenate([rows[:, i * depth : (i + 1) * depth] for i in range(chunks)], axis=0)
    pick = one_where(held == (iota((depth, bands * LANES), 0) + 1).astype(f32))
    picked = dot(stacked, pick, ((1,), (0,)))
    messages = jnp.zeros((ROWS, bands * LANES), f32)
    for i in range(chunks):
        messages = jnp.where(chunk == float(i), picked[i * ROWS : (i + 1) * ROWS], messages)
    flag_row = iota((ROWS, LANES), 0) == channels + 3
    for dest in range(bands):
        message = messages[:, dest * LANES : (dest + 1) * LANES]
        message = jnp.where(flag_row, overflow, message).astype(bf16)
        for level in range(levels):
            out_ref[level * bands + dest] = message
    for layer in layers:
        layer.wait()


def cheb_rows(colat):
    nodes = LAT_DEV
    x = jnp.broadcast_to(colat, (nodes, colat.shape[1]))
    node = iota((nodes, 1), 0).astype(f32)
    twice = x + x
    before, now = jnp.ones_like(x), x
    total = jnp.full_like(x, 1.0 / nodes)
    for order in range(1, nodes):
        scale = jnp.cos((math.pi * order / nodes) * (node + 0.5)) * (2.0 / nodes)
        total = total + now * scale
        before, now = now, twice * now - before
    return total


def gelu(x):
    slope = math.sqrt(2.0 / math.pi)
    half = 0.5 * x
    return half + half * jnp.tanh(x * (slope + (0.044715 * slope) * (x * x)))


def encode_kernel(
    bands, levels, channels,
    recv_ref, w_in_ref, b_in_ref, w_out_ref, b_out_ref, dct_ref, out_ref, flag_ref,
    spread_ref, spec_ref, turn_ref, done_ref, mark_ref, sems,
):
    modes = LAT_DEV * bands
    feats = levels * channels
    sub_lons = LON_DEV // SUBS
    lower = iota((ROWS, LANES), 1) < LANES // SUBS
    w_first = w_in_ref[...].astype(f32).T.astype(bf16)
    w_second = w_out_ref[...].astype(f32).T.astype(bf16)
    out_rows = w_second.shape[0]
    batch = max(1, sub_lons * LANES // modes)
    lane_tiles = batch * modes // LANES
    b_first = jnp.broadcast_to(b_in_ref[...], (LANES, b_in_ref.shape[1])).T
    b_second = jnp.broadcast_to(b_out_ref[...], (LANES, b_out_ref.shape[1])).T
    b_first = jnp.concatenate([b_first] * lane_tiles, axis=1)
    b_second = jnp.concatenate([b_second] * lane_tiles, axis=1)

    def half(level, sub):
        pieces = []
        for pair in range(bands // 2):
            even = recv_ref[level * bands + 2 * pair]
            odd = recv_ref[level * bands + 2 * pair + 1]
            pieces.append(jnp.where(lower, even, odd) if sub == 0 else jnp.where(lower, odd, even))
        return jnp.concatenate(pieces, axis=1)

    for sub in range(SUBS):
        parts = [half(level, sub) for level in range(levels)]
        meta = parts[0][channels:].astype(f32)
        values = jnp.concatenate([part[:channels] for part in parts], axis=0)
        lon, band, colat = meta[0:1], meta[1:2], meta[2:3]
        weight = cheb_rows(colat)
        nodes = jnp.concatenate(
            [jnp.where(band == float(b), weight, 0.0) for b in range(bands)], axis=0
        ).astype(bf16)
        basis = dot(dct_ref[...], nodes, ((1,), (0,))).astype(bf16)
        spread = spread_ref.at[sub % spread_ref.shape[0]]
        for m in range(sub_lons):
            here = one_where(lon == float(sub * sub_lons + m))
            spread[m * feats : (m + 1) * feats, :] = values * here
        spec_ref[sub] = dot(spread[...], basis, ((1,), (1,))).astype(bf16)

    flags = recv_ref[0, channels:, :].astype(f32)
    for source in range(1, levels * bands):
        flags = jnp.maximum(flags, recv_ref[source, channels:, :].astype(f32))
    mark_ref[0] = jnp.max(flags[3:4]).astype(jnp.int32)
    flag_ref[0] = mark_ref[0]
    copies = []
    for sub in range(SUBS):
        for first in range(0, sub_lons, batch):
            spectrum = jnp.concatenate(
                [spec_ref[sub, m * feats : (m + 1) * feats, :] for m in range(first, first + batch)],
                axis=1,
            )
            wide = spectrum.astype(f32)
            inv_norm = lax.rsqrt(
                jnp.sum(wide * wide, axis=0, keepdims=True) * (1.0 / feats) + norm_eps
            )
            pre_act = dot(w_first, spectrum, ((1,), (0,)))
            hidden = gelu(pre_act * inv_norm + b_first).astype(bf16)
            encoded = dot(w_second, hidden, ((1,), (0,))) + b_second
            for j in range(batch):
                for i in range(modes // LANES):
                    tile = j * (modes // LANES) + i
                    turn_ref[sub, i, pl.ds(first + j, out_rows, stride=sub_lons), :] = encoded[
                        :, tile * LANES : (tile + 1) * LANES
                    ]
        for i in range(modes // LANES):
            turned = turn_ref[sub, i].reshape(out_rows, sub_lons, LANES).astype(bf16)
            done_ref[sub, :, :, i * LANES : (i + 1) * LANES] = turned
        copy = pltpu.make_async_copy(
            done_ref.at[sub], out_ref.at[:, pl.ds(sub * sub_lons, sub_lons), :], sems.at[sub]
        )
        copy.start()
        copies.append(copy)
    for copy in copies:
        copy.wait()


def on_device(obs_vals, obs_colat, obs_lon, band_list, counts, w_in, b_in, w_out, b_out):
    bands = lax.axis_size("band")
    levels = lax.axis_size("lev")
    channels = obs_vals.shape[1]
    feats = levels * channels
    modes = LAT_DEV * bands
    sub_lons = LON_DEV // SUBS
    slots = bands * LANES // SUBS
    out_rows = w_out.shape[1]
    vmem = pl.BlockSpec(memory_space=pltpu.VMEM)
    smem = pl.BlockSpec(memory_space=pltpu.SMEM)

    hbm = pl.BlockSpec(memory_space=pltpu.HBM)
    obs = obs_lon.shape[0]
    layers = [w_in, b_in.reshape(1, -1), w_out, b_out.reshape(1, -1)]
    packed, *layers = pl.pallas_call(
        lambda *refs: pack_kernel(bands, levels, *refs),
        out_shape=[pltpu.VMEM((levels * bands, ROWS, LANES), bf16)]
        + [pltpu.VMEM(layer.shape, layer.dtype) for layer in layers]
        + [pltpu.VMEM((modes, modes), bf16)],
        in_specs=[hbm] * 9,
        out_specs=[vmem] * 6,
        scratch_shapes=[
            pltpu.SMEM((1, bands), jnp.int32),
            pltpu.VMEM((bands, LANES), jnp.int32),
            pltpu.VMEM((obs // LANES, LANES), jnp.int32),
            pltpu.VMEM((obs // LANES, LANES), bf16),
            pltpu.VMEM((channels, obs), bf16),
            pltpu.SemaphoreType.DMA((5,)),
            pltpu.SemaphoreType.DMA((4,)),
        ],
        compiler_params=pltpu.CompilerParams(vmem_limit_bytes=(16 if bands <= 16 else 48) << 20),
        name="pack",
    )(
        counts, band_list[0], obs_lon.reshape(-1, LANES), obs_colat.reshape(-1, LANES), obs_vals[0],
        *layers,
    )

    received = lax.all_to_all(packed, ("lev", "band"), split_axis=0, concat_axis=0, tiled=True)
    received = pltpu.with_memory_space_constraint(received, pltpu.VMEM)
    spread_buffers = SUBS if bands <= 16 else 1
    encoded, overflow = pl.pallas_call(
        lambda *refs: encode_kernel(bands, levels, channels, *refs),
        out_shape=[
            jax.ShapeDtypeStruct((out_rows, LON_DEV, modes), bf16),
            pltpu.SMEM((1,), jnp.int32),
        ],
        in_specs=[vmem] * 6,
        out_specs=[hbm, pl.BlockSpec(memory_space=pltpu.SMEM)],
        scratch_shapes=[
            pltpu.VMEM((spread_buffers, sub_lons * feats, slots), bf16),
            pltpu.VMEM((SUBS, sub_lons * feats, modes), bf16),
            pltpu.VMEM((SUBS, modes // LANES, out_rows * sub_lons, LANES), f32),
            pltpu.VMEM((SUBS, out_rows, sub_lons, modes), bf16),
            pltpu.SMEM((1,), jnp.int32),
            pltpu.SemaphoreType.DMA((SUBS + 1,)),
        ],
        compiler_params=pltpu.CompilerParams(vmem_limit_bytes=(24 if bands <= 16 else 56) << 20),
        name="encode",
    )(received, *layers)

    def by_bands():
        vals = whole_copy(obs_vals)
        return whole_copy(by_band(vals, obs_colat, obs_lon, band_list, counts, w_in, b_in, w_out, b_out))

    def again(carry):
        return by_bands(), jnp.zeros_like(carry[1])

    return lax.while_loop(lambda carry: carry[1], again, (encoded, overflow[0] > 0))[0]


def solution(mesh):
    in_specs = (
        P("lev", None, "band"),
        P("band"),
        P("band"),
        P("band", None, None),
        P("band", None),
        P(),
        P(),
        P(None, "lev"),
        P("lev"),
    )
    out_specs = P("lev", "band", None)
    return jax.shard_map(
        on_device, mesh=mesh, in_specs=in_specs, out_specs=out_specs, check_vma=False
    )
```

```python
import math

import jax
import jax.numpy as jnp
from jax import lax
from jax.experimental import pallas as pl
from jax.experimental.pallas import tpu as pltpu
from jax.sharding import PartitionSpec as P

LAT_DEV = 8
LON_DEV = 32
SUBS = 2
SPARE = 4
FIELD_ROWS = 16
FIELDS = 3
LANES = 128

norm_eps = 1e-05
bf16 = jnp.bfloat16
f32 = jnp.float32


def cheb_inverse(nodes):
    order_ids = jnp.arange(nodes, dtype=jnp.float32)[:, None]
    node_ids = jnp.arange(nodes, dtype=jnp.float32)[None, :]
    factor = jnp.where(order_ids == 0.0, 1.0, 2.0).astype(jnp.float32) / nodes
    return factor * jnp.cos(math.pi * order_ids * (node_ids + 0.5) / nodes)


def lat_weights(colat, nodes):
    angles = jnp.arccos(jnp.clip(colat, -1.0, 1.0))
    order_ids = jnp.arange(nodes, dtype=jnp.float32)
    cheb_terms = jnp.cos(order_ids[:, None] * angles[None, :])
    return jnp.dot(cheb_inverse(nodes).T, cheb_terms, precision=lax.Precision.HIGHEST)


def dct_table(length):
    mode_ids = jnp.arange(length, dtype=jnp.float32)[:, None]
    node_ids = jnp.arange(length, dtype=jnp.float32)[None, :]
    row_scale = jnp.where(mode_ids == 0.0, math.sqrt(1.0 / length), math.sqrt(2.0 / length)).astype(
        jnp.float32
    )
    return (row_scale * jnp.cos(math.pi * mode_ids * (node_ids + 0.5) / length)).astype(
        jnp.bfloat16
    )


def by_band(obs_vals, obs_colat, obs_lon, band_list, counts, w_in, b_in, w_out, b_out):
    band_count = lax.axis_size("band")
    capacity = band_list.shape[2]
    lat_nodes = LAT_DEV
    lon_local = LON_DEV
    lon_count = lon_local * band_count
    lat_total = lat_nodes * band_count
    channels = obs_vals.shape[1]
    feat_count = w_in.shape[0]
    picked = band_list[0].reshape(-1)
    live_slot = (jnp.arange(capacity, dtype=jnp.int32)[None, :] < counts[0][:, None]).reshape(-1)
    outgoing = jnp.where(
        live_slot[None, :], jnp.take(obs_vals[0], picked, axis=1), jnp.zeros((), jnp.bfloat16)
    )
    colat_out = jnp.take(obs_colat, picked)[None, :]
    lon_out = jnp.take(obs_lon, picked)[None, :]
    incoming, colat_in, lon_in = (
        lax.all_to_all(outgoing, "band", split_axis=1, concat_axis=1, tiled=True),
        lax.all_to_all(colat_out, "band", split_axis=1, concat_axis=1, tiled=True),
        lax.all_to_all(lon_out, "band", split_axis=1, concat_axis=1, tiled=True),
    )
    weights = lat_weights(colat_in[0].astype(jnp.float32), lat_nodes)
    weighted = (incoming.astype(jnp.float32)[:, None, :] * weights[None]).astype(jnp.bfloat16)
    weighted = weighted.reshape(channels * lat_nodes, -1)
    lon_ids = lon_in[0]
    row_count = weighted.shape[1]
    block_rows = math.gcd(row_count, 1024)
    columns = jnp.arange(lon_count, dtype=jnp.int32)

    def add_block(step_index, grid_sum):
        first_row = step_index * block_rows
        block_vals = lax.dynamic_slice_in_dim(weighted, first_row, block_rows, 1)
        block_lon = lax.dynamic_slice_in_dim(lon_ids, first_row, block_rows, 0)
        onehot = (block_lon[:, None] == columns[None, :]).astype(jnp.bfloat16)
        return grid_sum + jnp.dot(block_vals, onehot, preferred_element_type=jnp.float32)

    grid_sum = lax.fori_loop(
        0,
        row_count // block_rows,
        add_block,
        jnp.zeros((channels * lat_nodes, lon_count), jnp.float32),
    )
    grid_half = grid_sum.astype(jnp.bfloat16).reshape(channels, lat_nodes, lon_count)
    received = lax.all_to_all(grid_half, "band", split_axis=2, concat_axis=2, tiled=True)
    items = received.shape[0]
    arranged = received.reshape(items, lat_nodes, band_count, lon_local)
    table = dct_table(lat_total).reshape(lat_total, band_count, lat_nodes)
    spectrum = jnp.einsum(
        "cjbm,kbj->cmk", arranged, table, preferred_element_type=jnp.float32
    ).astype(jnp.bfloat16)
    shard_rows = lax.all_gather(spectrum, "lev", axis=0, tiled=True)
    pre_act = jnp.einsum("fh,fmk->hmk", w_in, shard_rows, preferred_element_type=jnp.float32)
    squared = shard_rows.astype(jnp.float32)
    pre_act, sum_sq = (pre_act, jnp.sum(squared * squared, axis=0))
    inv_norm = lax.rsqrt(sum_sq * (1.0 / feat_count) + norm_eps)
    hidden = jax.nn.gelu(pre_act * inv_norm[None] + b_in[:, None, None]).astype(jnp.bfloat16)
    output = (
        jnp.einsum("ho,hmk->omk", w_out, hidden, preferred_element_type=jnp.float32)
        + b_out[:, None, None]
    )
    return output.astype(jnp.bfloat16)


def dot(lhs, rhs, contract):
    return lax.dot_general(lhs, rhs, (contract, ((), ())), preferred_element_type=f32)


def iota(shape, dim):
    return lax.broadcasted_iota(jnp.int32, shape, dim)


def one_where(mask):
    return jnp.where(mask, 1.0, 0.0).astype(bf16)


def cosine_rows(length):
    mode = iota((length, length), 0)
    angle = (mode * (2 * iota((length, length), 1) + 1)) & (4 * length - 1)
    scale = jnp.where(mode == 0, math.sqrt(1.0 / length), math.sqrt(2.0 / length))
    return (scale * jnp.cos(angle.astype(f32) * (math.pi / (2 * length)))).astype(bf16)


def spare_lanes():
    half = LANES // SUBS
    source, target = iota((LANES, LANES), 0), iota((LANES, LANES), 1)
    return one_where(
        ((source & (half - 1)) >= half - SPARE)
        & (source // half == target // half)
        & ((source & (SPARE - 1)) == (target & (SPARE - 1)))
    )


def row_of(tiles):
    return jnp.concatenate([tiles[i : i + 1] for i in range(tiles.shape[0])], axis=1)


def whole_copy(array):
    def kernel(from_ref, to_ref, sem):
        copy = pltpu.make_async_copy(from_ref, to_ref, sem)
        copy.start()
        copy.wait()

    hbm = pl.BlockSpec(memory_space=pltpu.HBM)
    return pl.pallas_call(
        kernel,
        out_shape=jax.ShapeDtypeStruct(array.shape, array.dtype),
        in_specs=[hbm],
        out_specs=hbm,
        scratch_shapes=[pltpu.SemaphoreType.DMA],
        name="whole_copy",
    )(array)


def pack_kernel(bands, levels, *refs):
    counts_hbm, list_hbm, lon_hbm, colat_hbm, vals_hbm = refs[:5]
    layers_hbm, out_ref, layers_ref, dct_ref = refs[5:9], refs[9], refs[10:14], refs[14]
    counts_ref, list_ref, lon_ref, colat_ref, vals_ref, in_sems, layer_sems = refs[15:]
    loads = [
        pltpu.make_async_copy(source, target, in_sems.at[i])
        for i, (source, target) in enumerate(
            [
                (counts_hbm, counts_ref),
                (list_hbm, list_ref),
                (lon_hbm, lon_ref),
                (colat_hbm, colat_ref),
                (vals_hbm, vals_ref),
            ]
        )
    ]
    layers = [
        pltpu.make_async_copy(source, target, layer_sems.at[i])
        for i, (source, target) in enumerate(zip(layers_hbm, layers_ref))
    ]
    for load in loads + layers:
        load.start()
    dct_ref[...] = cosine_rows(dct_ref.shape[0])
    for load in loads:
        load.wait()
    channels, obs = vals_ref.shape
    blocks = obs // LANES
    low_parts, high_parts = [], []
    for band in range(bands):
        entry = list_ref[band : band + 1, :]
        entry = jnp.where(iota((1, LANES), 1) < counts_ref[0, band], entry, -1)
        high_parts.append(jnp.where((entry >> 7) == iota((blocks, LANES), 0), float(band), 0.0))
        low_parts.append(one_where((entry & 127) == iota((LANES, LANES), 0)))
    high = jnp.concatenate(high_parts, axis=1).astype(bf16)
    low = jnp.concatenate(low_parts, axis=1)
    band_row = row_of(dot(high, low, ((1,), (1,))))

    lon = row_of(lon_ref[...])
    sub_lons = LON_DEV // SUBS
    cap = LANES // SUBS - SPARE
    groups = bands * SUBS
    odd = lax.axis_index("band") & 1
    group = (lon // sub_lons) ^ odd
    member = jnp.where(group == iota((groups, obs), 0), 1.0, 0.0)
    earlier = one_where(iota((LANES, LANES), 0) < iota((LANES, LANES), 1))
    carry = jnp.zeros((groups, 1), f32)
    places = []
    for i in range(blocks):
        part = member[:, i * LANES : (i + 1) * LANES]
        before = dot(part.astype(bf16), earlier, ((1,), (0,))) + carry
        places.append(jnp.sum(part * before, axis=0, keepdims=True))
        carry = carry + jnp.sum(part, axis=1, keepdims=True)
    place = jnp.concatenate(places, axis=1).astype(jnp.int32)
    overflow = jnp.where(jnp.max(carry) > cap, 1.0, 0.0)
    slot = jnp.where(place < cap, group * (LANES // SUBS) + place, -1)

    depth = 2 * LANES
    chunks = obs // depth
    number = iota((1, obs), 1)
    mine = (slot >> 7) == iota((bands, obs), 0)
    held = jnp.where(mine, ((number & (depth - 1)) + 1).astype(f32), 0.0)
    chunk = jnp.where(mine, (number // depth).astype(f32), 0.0)
    lane = one_where((slot & (LANES - 1)) == iota((LANES, obs), 0))
    found = dot(jnp.concatenate([held, chunk], axis=0).astype(bf16), lane, ((1,), (1,)))
    held, chunk = row_of(found[:bands]), row_of(found[bands:])

    row_count = -(-(channels + FIELDS) // 16) * 16
    rows = jnp.concatenate(
        [
            vals_ref[...].astype(f32),
            (lon & (LON_DEV - 1)).astype(f32),
            band_row,
            row_of(colat_ref[...].astype(f32)),
            jnp.zeros((row_count - channels - FIELDS, obs), f32),
        ],
        axis=0,
    ).astype(bf16)
    stacked = jnp.concatenate([rows[:, i * depth : (i + 1) * depth] for i in range(chunks)], axis=0)
    pick = one_where(held == (iota((depth, bands * LANES), 0) + 1).astype(f32))
    picked = dot(stacked, pick, ((1,), (0,)))
    found = jnp.zeros((row_count, bands * LANES), f32)
    for i in range(chunks):
        found = jnp.where(chunk == float(i), picked[i * row_count : (i + 1) * row_count], found)

    half_lane = iota((channels, bands * LANES), 1) & (LANES // SUBS - 1)
    row = iota((channels, bands * LANES), 0) + lax.axis_index("lev") * channels
    lon_row, band_row, colat_row = (found[channels + i : channels + i + 1] for i in range(FIELDS))
    lon_row = jnp.where(half_lane[:1] >= cap, overflow, lon_row)
    field = jnp.where(row < FIELD_ROWS, lon_row, jnp.where(row < 2 * FIELD_ROWS, band_row, colat_row))
    wanted = (half_lane // SPARE == (row & (FIELD_ROWS - 1))) & (row < FIELDS * FIELD_ROWS)
    field = jnp.where(wanted, field, 0.0)
    tiles = [slice(dest * LANES, (dest + 1) * LANES) for dest in range(bands)]
    field = jnp.concatenate([field[:, tile] for tile in tiles], axis=0).astype(bf16)
    field = dot(field, spare_lanes(), ((1,), (1,)))
    for dest in range(bands):
        message = found[:channels, tiles[dest]] + field[dest * channels : (dest + 1) * channels]
        for level in range(levels):
            out_ref[level * bands + dest] = message.astype(bf16)
    for layer in layers:
        layer.wait()


def cheb_rows(colat):
    nodes = LAT_DEV
    x = jnp.broadcast_to(colat, (nodes, colat.shape[1]))
    node = iota((nodes, 1), 0).astype(f32)
    twice = x + x
    before, now = jnp.ones_like(x), x
    total = jnp.full_like(x, 1.0 / nodes)
    for order in range(1, nodes):
        scale = jnp.cos((math.pi * order / nodes) * (node + 0.5)) * (2.0 / nodes)
        total = total + now * scale
        before, now = now, twice * now - before
    return total


def gelu(x):
    slope = math.sqrt(2.0 / math.pi)
    half = 0.5 * x
    return half + half * jnp.tanh(x * (slope + (0.044715 * slope) * (x * x)))


def encode_kernel(
    bands, levels, channels,
    recv_ref, w_in_ref, b_in_ref, w_out_ref, b_out_ref, dct_ref, out_ref, flag_ref,
    spread_ref, spec_ref, turn_ref, done_ref, sems,
):
    modes = LAT_DEV * bands
    feats = levels * channels
    sub_lons = LON_DEV // SUBS
    lower = iota((channels, LANES), 1) < LANES // SUBS
    w_first = w_in_ref[...].astype(f32).T.astype(bf16)
    w_second = w_out_ref[...].astype(f32).T.astype(bf16)
    out_rows = w_second.shape[0]
    batch = max(1, sub_lons * LANES // modes)
    lane_tiles = batch * modes // LANES
    b_first = jnp.broadcast_to(b_in_ref[...], (LANES, b_in_ref.shape[1])).T
    b_second = jnp.broadcast_to(b_out_ref[...], (LANES, b_out_ref.shape[1])).T
    b_first = jnp.concatenate([b_first] * lane_tiles, axis=1)
    b_second = jnp.concatenate([b_second] * lane_tiles, axis=1)

    def half(level, sub):
        pieces = []
        for pair in range(bands // 2):
            even = recv_ref[level * bands + 2 * pair]
            odd = recv_ref[level * bands + 2 * pair + 1]
            pieces.append(jnp.where(lower, even, odd) if sub == 0 else jnp.where(lower, odd, even))
        return jnp.concatenate(pieces, axis=1)

    slots = bands * LANES // SUBS
    carriers = -(-FIELDS * FIELD_ROWS // channels)
    half_lane = iota((FIELD_ROWS, slots), 1) & (LANES // SUBS - 1)
    wanted = half_lane // SPARE == iota((FIELD_ROWS, slots), 0)
    unused = half_lane[:1] >= LANES // SUBS - SPARE
    flags = []
    for sub in range(SUBS):
        parts = [half(level, sub) for level in range(levels)]
        values = jnp.concatenate(parts, axis=0)
        wide = jnp.concatenate([part.astype(f32) for part in parts[:carriers]], axis=0)
        wide = wide[: FIELDS * FIELD_ROWS]
        tiles = [wide[:, i * LANES : (i + 1) * LANES] for i in range(slots // LANES)]
        fields = dot(jnp.concatenate(tiles, axis=0).astype(bf16), spare_lanes(), ((1,), (0,)))
        fields = jnp.concatenate(
            [fields[i * wide.shape[0] : (i + 1) * wide.shape[0]] for i in range(len(tiles))], axis=1
        )
        lon, band, colat = (
            jnp.sum(
                jnp.where(wanted, fields[i * FIELD_ROWS : (i + 1) * FIELD_ROWS], 0.0),
                axis=0,
                keepdims=True,
            )
            for i in range(FIELDS)
        )
        flags.append(jnp.where(unused, lon, 0.0))
        lon = jnp.where(unused, -1.0, lon)
        weight = cheb_rows(colat)
        nodes = jnp.concatenate(
            [jnp.where(band == float(b), weight, 0.0) for b in range(bands)], axis=0
        ).astype(bf16)
        basis = dot(dct_ref[...], nodes, ((1,), (0,))).astype(bf16)
        spread = spread_ref.at[sub % spread_ref.shape[0]]
        for m in range(sub_lons):
            here = one_where(lon == float(sub * sub_lons + m))
            spread[m * feats : (m + 1) * feats, :] = values * here
        spec_ref[sub] = dot(spread[...], basis, ((1,), (1,))).astype(bf16)

    flag_ref[0] = jnp.max(jnp.maximum(*flags)).astype(jnp.int32)
    copies = []
    for sub in range(SUBS):
        for first in range(0, sub_lons, batch):
            spectrum = jnp.concatenate(
                [spec_ref[sub, m * feats : (m + 1) * feats, :] for m in range(first, first + batch)],
                axis=1,
            )
            wide = spectrum.astype(f32)
            inv_norm = lax.rsqrt(
                jnp.sum(wide * wide, axis=0, keepdims=True) * (1.0 / feats) + norm_eps
            )
            pre_act = dot(w_first, spectrum, ((1,), (0,)))
            hidden = gelu(pre_act * inv_norm + b_first).astype(bf16)
            encoded = dot(w_second, hidden, ((1,), (0,))) + b_second
            for j in range(batch):
                for i in range(modes // LANES):
                    tile = j * (modes // LANES) + i
                    turn_ref[sub, i, pl.ds(first + j, out_rows, stride=sub_lons), :] = encoded[
                        :, tile * LANES : (tile + 1) * LANES
                    ]
        for i in range(modes // LANES):
            turned = turn_ref[sub, i].reshape(out_rows, sub_lons, LANES).astype(bf16)
            done_ref[sub, :, :, i * LANES : (i + 1) * LANES] = turned
        copy = pltpu.make_async_copy(
            done_ref.at[sub], out_ref.at[:, pl.ds(sub * sub_lons, sub_lons), :], sems.at[sub]
        )
        copy.start()
        copies.append(copy)
    for copy in copies:
        copy.wait()


def on_device(obs_vals, obs_colat, obs_lon, band_list, counts, w_in, b_in, w_out, b_out):
    bands = lax.axis_size("band")
    levels = lax.axis_size("lev")
    channels = obs_vals.shape[1]
    feats = levels * channels
    modes = LAT_DEV * bands
    sub_lons = LON_DEV // SUBS
    slots = bands * LANES // SUBS
    out_rows = w_out.shape[1]
    vmem = pl.BlockSpec(memory_space=pltpu.VMEM)
    smem = pl.BlockSpec(memory_space=pltpu.SMEM)

    hbm = pl.BlockSpec(memory_space=pltpu.HBM)
    obs = obs_lon.shape[0]
    layers = [w_in, b_in.reshape(1, -1), w_out, b_out.reshape(1, -1)]
    packed, *layers = pl.pallas_call(
        lambda *refs: pack_kernel(bands, levels, *refs),
        out_shape=[pltpu.VMEM((levels * bands, channels, LANES), bf16)]
        + [pltpu.VMEM(layer.shape, layer.dtype) for layer in layers]
        + [pltpu.VMEM((modes, modes), bf16)],
        in_specs=[hbm] * 9,
        out_specs=[vmem] * 6,
        scratch_shapes=[
            pltpu.SMEM((1, bands), jnp.int32),
            pltpu.VMEM((bands, LANES), jnp.int32),
            pltpu.VMEM((obs // LANES, LANES), jnp.int32),
            pltpu.VMEM((obs // LANES, LANES), bf16),
            pltpu.VMEM((channels, obs), bf16),
            pltpu.SemaphoreType.DMA((5,)),
            pltpu.SemaphoreType.DMA((4,)),
        ],
        compiler_params=pltpu.CompilerParams(vmem_limit_bytes=(16 if bands <= 16 else 48) << 20),
        name="pack",
    )(
        counts, band_list[0], obs_lon.reshape(-1, LANES), obs_colat.reshape(-1, LANES), obs_vals[0],
        *layers,
    )

    received = lax.all_to_all(packed, ("lev", "band"), split_axis=0, concat_axis=0, tiled=True)
    received = pltpu.with_memory_space_constraint(received, pltpu.VMEM)
    spread_buffers = SUBS if bands <= 16 else 1
    encoded, overflow = pl.pallas_call(
        lambda *refs: encode_kernel(bands, levels, channels, *refs),
        out_shape=[
            jax.ShapeDtypeStruct((out_rows, LON_DEV, modes), bf16),
            pltpu.SMEM((1,), jnp.int32),
        ],
        in_specs=[vmem] * 6,
        out_specs=[hbm, pl.BlockSpec(memory_space=pltpu.SMEM)],
        scratch_shapes=[
            pltpu.VMEM((spread_buffers, sub_lons * feats, slots), bf16),
            pltpu.VMEM((SUBS, sub_lons * feats, modes), bf16),
            pltpu.VMEM((SUBS, modes // LANES, out_rows * sub_lons, LANES), f32),
            pltpu.VMEM((SUBS, out_rows, sub_lons, modes), bf16),
            pltpu.SemaphoreType.DMA((SUBS,)),
        ],
        compiler_params=pltpu.CompilerParams(vmem_limit_bytes=(24 if bands <= 16 else 56) << 20),
        name="encode",
    )(received, *layers)

    def by_bands():
        vals = whole_copy(obs_vals)
        return whole_copy(by_band(vals, obs_colat, obs_lon, band_list, counts, w_in, b_in, w_out, b_out))

    def again(carry):
        return by_bands(), jnp.zeros_like(carry[1])

    return lax.while_loop(lambda carry: carry[1], again, (encoded, overflow[0] > 0))[0]


def solution(mesh):
    in_specs = (
        P("lev", None, "band"),
        P("band"),
        P("band"),
        P("band", None, None),
        P("band", None),
        P(),
        P(),
        P(None, "lev"),
        P("lev"),
    )
    out_specs = P("lev", "band", None)
    return jax.shard_map(
        on_device, mesh=mesh, in_specs=in_specs, out_specs=out_specs, check_vma=False
    )
```

```python
import math

import jax
import jax.numpy as jnp
from jax import lax
from jax.experimental import pallas as pl
from jax.experimental.pallas import tpu as pltpu
from jax.sharding import PartitionSpec as P

LAT_DEV = 8
LON_DEV = 32
SUBS = 2
SPARE = 4
FIELD_ROWS = 16
FIELDS = 3
LANES = 128

norm_eps = 1e-05
bf16 = jnp.bfloat16
f32 = jnp.float32


def cheb_inverse(nodes):
    order_ids = jnp.arange(nodes, dtype=jnp.float32)[:, None]
    node_ids = jnp.arange(nodes, dtype=jnp.float32)[None, :]
    factor = jnp.where(order_ids == 0.0, 1.0, 2.0).astype(jnp.float32) / nodes
    return factor * jnp.cos(math.pi * order_ids * (node_ids + 0.5) / nodes)


def lat_weights(colat, nodes):
    angles = jnp.arccos(jnp.clip(colat, -1.0, 1.0))
    order_ids = jnp.arange(nodes, dtype=jnp.float32)
    cheb_terms = jnp.cos(order_ids[:, None] * angles[None, :])
    return jnp.dot(cheb_inverse(nodes).T, cheb_terms, precision=lax.Precision.HIGHEST)


def dct_table(length):
    mode_ids = jnp.arange(length, dtype=jnp.float32)[:, None]
    node_ids = jnp.arange(length, dtype=jnp.float32)[None, :]
    row_scale = jnp.where(mode_ids == 0.0, math.sqrt(1.0 / length), math.sqrt(2.0 / length)).astype(
        jnp.float32
    )
    return (row_scale * jnp.cos(math.pi * mode_ids * (node_ids + 0.5) / length)).astype(
        jnp.bfloat16
    )


def by_band(obs_vals, obs_colat, obs_lon, band_list, counts, w_in, b_in, w_out, b_out):
    band_count = lax.axis_size("band")
    capacity = band_list.shape[2]
    lat_nodes = LAT_DEV
    lon_local = LON_DEV
    lon_count = lon_local * band_count
    lat_total = lat_nodes * band_count
    channels = obs_vals.shape[1]
    feat_count = w_in.shape[0]
    picked = band_list[0].reshape(-1)
    live_slot = (jnp.arange(capacity, dtype=jnp.int32)[None, :] < counts[0][:, None]).reshape(-1)
    outgoing = jnp.where(
        live_slot[None, :], jnp.take(obs_vals[0], picked, axis=1), jnp.zeros((), jnp.bfloat16)
    )
    colat_out = jnp.take(obs_colat, picked)[None, :]
    lon_out = jnp.take(obs_lon, picked)[None, :]
    incoming, colat_in, lon_in = (
        lax.all_to_all(outgoing, "band", split_axis=1, concat_axis=1, tiled=True),
        lax.all_to_all(colat_out, "band", split_axis=1, concat_axis=1, tiled=True),
        lax.all_to_all(lon_out, "band", split_axis=1, concat_axis=1, tiled=True),
    )
    weights = lat_weights(colat_in[0].astype(jnp.float32), lat_nodes)
    weighted = (incoming.astype(jnp.float32)[:, None, :] * weights[None]).astype(jnp.bfloat16)
    weighted = weighted.reshape(channels * lat_nodes, -1)
    lon_ids = lon_in[0]
    row_count = weighted.shape[1]
    block_rows = math.gcd(row_count, 1024)
    columns = jnp.arange(lon_count, dtype=jnp.int32)

    def add_block(step_index, grid_sum):
        first_row = step_index * block_rows
        block_vals = lax.dynamic_slice_in_dim(weighted, first_row, block_rows, 1)
        block_lon = lax.dynamic_slice_in_dim(lon_ids, first_row, block_rows, 0)
        onehot = (block_lon[:, None] == columns[None, :]).astype(jnp.bfloat16)
        return grid_sum + jnp.dot(block_vals, onehot, preferred_element_type=jnp.float32)

    grid_sum = lax.fori_loop(
        0,
        row_count // block_rows,
        add_block,
        jnp.zeros((channels * lat_nodes, lon_count), jnp.float32),
    )
    grid_half = grid_sum.astype(jnp.bfloat16).reshape(channels, lat_nodes, lon_count)
    received = lax.all_to_all(grid_half, "band", split_axis=2, concat_axis=2, tiled=True)
    items = received.shape[0]
    arranged = received.reshape(items, lat_nodes, band_count, lon_local)
    table = dct_table(lat_total).reshape(lat_total, band_count, lat_nodes)
    spectrum = jnp.einsum(
        "cjbm,kbj->cmk", arranged, table, preferred_element_type=jnp.float32
    ).astype(jnp.bfloat16)
    shard_rows = lax.all_gather(spectrum, "lev", axis=0, tiled=True)
    pre_act = jnp.einsum("fh,fmk->hmk", w_in, shard_rows, preferred_element_type=jnp.float32)
    squared = shard_rows.astype(jnp.float32)
    pre_act, sum_sq = (pre_act, jnp.sum(squared * squared, axis=0))
    inv_norm = lax.rsqrt(sum_sq * (1.0 / feat_count) + norm_eps)
    hidden = jax.nn.gelu(pre_act * inv_norm[None] + b_in[:, None, None]).astype(jnp.bfloat16)
    output = (
        jnp.einsum("ho,hmk->omk", w_out, hidden, preferred_element_type=jnp.float32)
        + b_out[:, None, None]
    )
    return output.astype(jnp.bfloat16)


def dot(lhs, rhs, contract):
    return lax.dot_general(lhs, rhs, (contract, ((), ())), preferred_element_type=f32)


def iota(shape, dim):
    return lax.broadcasted_iota(jnp.int32, shape, dim)


def one_where(mask):
    return jnp.where(mask, 1.0, 0.0).astype(bf16)


def cosine_rows(length):
    mode = iota((length, length), 0)
    angle = (mode * (2 * iota((length, length), 1) + 1)) & (4 * length - 1)
    scale = jnp.where(mode == 0, math.sqrt(1.0 / length), math.sqrt(2.0 / length))
    return (scale * jnp.cos(angle.astype(f32) * (math.pi / (2 * length)))).astype(bf16)


def spare_lanes():
    half = LANES // SUBS
    source, target = iota((LANES, LANES), 0), iota((LANES, LANES), 1)
    return one_where(
        ((source & (half - 1)) >= half - SPARE)
        & (source // half == target // half)
        & ((source & (SPARE - 1)) == (target & (SPARE - 1)))
    )


def row_of(tiles):
    return jnp.concatenate([tiles[i : i + 1] for i in range(tiles.shape[0])], axis=1)


def whole_copy(array):
    def kernel(from_ref, to_ref, sem):
        copy = pltpu.make_async_copy(from_ref, to_ref, sem)
        copy.start()
        copy.wait()

    hbm = pl.BlockSpec(memory_space=pltpu.HBM)
    return pl.pallas_call(
        kernel,
        out_shape=jax.ShapeDtypeStruct(array.shape, array.dtype),
        in_specs=[hbm],
        out_specs=hbm,
        scratch_shapes=[pltpu.SemaphoreType.DMA],
        name="whole_copy",
    )(array)


def pack_kernel(bands, levels, *refs):
    counts_hbm, list_hbm, lon_hbm, colat_hbm, vals_hbm = refs[:5]
    layers_hbm, out_ref, layers_ref, dct_ref = refs[5:9], refs[9], refs[10:14], refs[14]
    counts_ref, list_ref, lon_ref, colat_ref, vals_ref, in_sems, layer_sems = refs[15:]
    loads = [
        pltpu.make_async_copy(source, target, in_sems.at[i])
        for i, (source, target) in enumerate(
            [
                (counts_hbm, counts_ref),
                (list_hbm, list_ref),
                (lon_hbm, lon_ref),
                (colat_hbm, colat_ref),
                (vals_hbm, vals_ref),
            ]
        )
    ]
    layers = [
        pltpu.make_async_copy(source, target, layer_sems.at[i])
        for i, (source, target) in enumerate(zip(layers_hbm, layers_ref))
    ]
    for load in loads + layers:
        load.start()
    dct_ref[...] = cosine_rows(dct_ref.shape[0])
    for load in loads[:3]:
        load.wait()
    channels, obs = vals_ref.shape
    blocks = obs // LANES
    low_parts, high_parts = [], []
    for band in range(bands):
        entry = list_ref[band : band + 1, :]
        entry = jnp.where(iota((1, LANES), 1) < counts_ref[0, band], entry, -1)
        high_parts.append(jnp.where((entry >> 7) == iota((blocks, LANES), 0), float(band), 0.0))
        low_parts.append(one_where((entry & 127) == iota((LANES, LANES), 0)))
    high = jnp.concatenate(high_parts, axis=1).astype(bf16)
    low = jnp.concatenate(low_parts, axis=1)
    band_row = row_of(dot(high, low, ((1,), (1,))))

    lon = row_of(lon_ref[...])
    sub_lons = LON_DEV // SUBS
    cap = LANES // SUBS - SPARE
    groups = bands * SUBS
    odd = lax.axis_index("band") & 1
    group = (lon // sub_lons) ^ odd
    member = jnp.where(group == iota((groups, obs), 0), 1.0, 0.0)
    earlier = one_where(iota((LANES, LANES), 0) < iota((LANES, LANES), 1))
    carry = jnp.zeros((groups, 1), f32)
    places = []
    for i in range(blocks):
        part = member[:, i * LANES : (i + 1) * LANES]
        before = dot(part.astype(bf16), earlier, ((1,), (0,))) + carry
        places.append(jnp.sum(part * before, axis=0, keepdims=True))
        carry = carry + jnp.sum(part, axis=1, keepdims=True)
    place = jnp.concatenate(places, axis=1).astype(jnp.int32)
    overflow = jnp.where(jnp.max(carry) > cap, 1.0, 0.0)
    slot = jnp.where(place < cap, group * (LANES // SUBS) + place, -1)

    depth = 2 * LANES
    chunks = obs // depth
    number = iota((1, obs), 1)
    mine = (slot >> 7) == iota((bands, obs), 0)
    held = jnp.where(mine, ((number & (depth - 1)) + 1).astype(f32), 0.0)
    chunk = jnp.where(mine, (number // depth).astype(f32), 0.0)
    lane = one_where((slot & (LANES - 1)) == iota((LANES, obs), 0))
    found = dot(jnp.concatenate([held, chunk], axis=0).astype(bf16), lane, ((1,), (1,)))
    held, chunk = row_of(found[:bands]), row_of(found[bands:])

    row_count = -(-(channels + FIELDS) // 16) * 16
    for load in loads[3:]:
        load.wait()
    rows = jnp.concatenate(
        [
            vals_ref[...].astype(f32),
            (lon & (LON_DEV - 1)).astype(f32),
            band_row,
            row_of(colat_ref[...].astype(f32)),
            jnp.zeros((row_count - channels - FIELDS, obs), f32),
        ],
        axis=0,
    ).astype(bf16)
    stacked = jnp.concatenate([rows[:, i * depth : (i + 1) * depth] for i in range(chunks)], axis=0)
    pick = one_where(held == (iota((depth, bands * LANES), 0) + 1).astype(f32))
    picked = dot(stacked, pick, ((1,), (0,)))
    found = jnp.zeros((row_count, bands * LANES), f32)
    for i in range(chunks):
        found = jnp.where(chunk == float(i), picked[i * row_count : (i + 1) * row_count], found)

    half_lane = iota((channels, bands * LANES), 1) & (LANES // SUBS - 1)
    row = iota((channels, bands * LANES), 0) + lax.axis_index("lev") * channels
    lon_row, band_row, colat_row = (found[channels + i : channels + i + 1] for i in range(FIELDS))
    lon_row = jnp.where(half_lane[:1] >= cap, overflow, lon_row)
    field = jnp.where(row < FIELD_ROWS, lon_row, jnp.where(row < 2 * FIELD_ROWS, band_row, colat_row))
    wanted = (half_lane // SPARE == (row & (FIELD_ROWS - 1))) & (row < FIELDS * FIELD_ROWS)
    field = jnp.where(wanted, field, 0.0)
    tiles = [slice(dest * LANES, (dest + 1) * LANES) for dest in range(bands)]
    field = jnp.concatenate([field[:, tile] for tile in tiles], axis=0).astype(bf16)
    field = dot(field, spare_lanes(), ((1,), (1,)))
    for dest in range(bands):
        message = found[:channels, tiles[dest]] + field[dest * channels : (dest + 1) * channels]
        for level in range(levels):
            out_ref[level * bands + dest] = message.astype(bf16)
    for layer in layers:
        layer.wait()


def cheb_rows(colat):
    nodes = LAT_DEV
    x = jnp.broadcast_to(colat, (nodes, colat.shape[1]))
    node = iota((nodes, 1), 0).astype(f32)
    twice = x + x
    before, now = jnp.ones_like(x), x
    total = jnp.full_like(x, 1.0 / nodes)
    for order in range(1, nodes):
        scale = jnp.cos((math.pi * order / nodes) * (node + 0.5)) * (2.0 / nodes)
        total = total + now * scale
        before, now = now, twice * now - before
    return total


def gelu_of_twice(half):
    slope = math.sqrt(2.0 / math.pi)
    return half + half * jnp.tanh(half * (2.0 * slope + (8.0 * 0.044715 * slope) * (half * half)))


def encode_kernel(
    bands, levels, channels,
    recv_ref, w_in_ref, b_in_ref, w_out_ref, b_out_ref, dct_ref, out_ref, flag_ref,
    spread_ref, spec_ref, turn_ref, done_ref, sems,
):
    modes = LAT_DEV * bands
    feats = levels * channels
    sub_lons = LON_DEV // SUBS
    lower = iota((channels, LANES), 1) < LANES // SUBS
    w_first = w_in_ref[...].astype(f32).T.astype(bf16)
    w_second = w_out_ref[...].astype(f32).T.astype(bf16)
    out_rows = w_second.shape[0]
    batch = max(1, sub_lons * LANES // modes)
    lane_tiles = batch * modes // LANES
    b_first = jnp.broadcast_to(0.5 * b_in_ref[...], (LANES, b_in_ref.shape[1])).T
    b_second = jnp.broadcast_to(b_out_ref[...], (LANES, b_out_ref.shape[1])).T
    b_first = jnp.concatenate([b_first] * lane_tiles, axis=1)
    b_second = jnp.concatenate([b_second] * lane_tiles, axis=1)

    def half(level, sub):
        pieces = []
        for pair in range(bands // 2):
            even = recv_ref[level * bands + 2 * pair]
            odd = recv_ref[level * bands + 2 * pair + 1]
            pieces.append(jnp.where(lower, even, odd) if sub == 0 else jnp.where(lower, odd, even))
        return jnp.concatenate(pieces, axis=1)

    slots = bands * LANES // SUBS
    carriers = -(-FIELDS * FIELD_ROWS // channels)
    half_lane = iota((FIELD_ROWS, slots), 1) & (LANES // SUBS - 1)
    wanted = half_lane // SPARE == iota((FIELD_ROWS, slots), 0)
    unused = half_lane[:1] >= LANES // SUBS - SPARE
    flags = []
    for sub in range(SUBS):
        parts = [half(level, sub) for level in range(levels)]
        values = jnp.concatenate(parts, axis=0)
        wide = jnp.concatenate([part.astype(f32) for part in parts[:carriers]], axis=0)
        wide = wide[: FIELDS * FIELD_ROWS]
        tiles = [wide[:, i * LANES : (i + 1) * LANES] for i in range(slots // LANES)]
        fields = dot(jnp.concatenate(tiles, axis=0).astype(bf16), spare_lanes(), ((1,), (0,)))
        fields = jnp.concatenate(
            [fields[i * wide.shape[0] : (i + 1) * wide.shape[0]] for i in range(len(tiles))], axis=1
        )
        lon, band, colat = (
            jnp.sum(
                jnp.where(wanted, fields[i * FIELD_ROWS : (i + 1) * FIELD_ROWS], 0.0),
                axis=0,
                keepdims=True,
            )
            for i in range(FIELDS)
        )
        flags.append(jnp.where(unused, lon, 0.0))
        lon = jnp.where(unused, -1.0, lon)
        weight = cheb_rows(colat)
        nodes = jnp.concatenate(
            [jnp.where(band == float(b), weight, 0.0) for b in range(bands)], axis=0
        ).astype(bf16)
        basis = dot(dct_ref[...], nodes, ((1,), (0,))).astype(bf16)
        spread = spread_ref.at[sub % spread_ref.shape[0]]
        for m in range(sub_lons):
            here = one_where(lon == float(sub * sub_lons + m))
            spread[m * feats : (m + 1) * feats, :] = values * here
        spec_ref[sub] = dot(spread[...], basis, ((1,), (1,))).astype(bf16)

    flag_ref[0] = jnp.max(jnp.maximum(*flags)).astype(jnp.int32)
    copies = []
    for sub in range(SUBS):
        for first in range(0, sub_lons, batch):
            spectrum = jnp.concatenate(
                [spec_ref[sub, m * feats : (m + 1) * feats, :] for m in range(first, first + batch)],
                axis=1,
            )
            wide = spectrum.astype(f32)
            inv_norm = lax.rsqrt(
                jnp.sum(wide * wide, axis=0, keepdims=True) * (1.0 / feats) + norm_eps
            )
            pre_act = dot(w_first, spectrum, ((1,), (0,)))
            hidden = gelu_of_twice(pre_act * (0.5 * inv_norm) + b_first).astype(bf16)
            encoded = dot(w_second, hidden, ((1,), (0,))) + b_second
            for j in range(batch):
                for i in range(modes // LANES):
                    tile = j * (modes // LANES) + i
                    turn_ref[sub, i, pl.ds(first + j, out_rows, stride=sub_lons), :] = encoded[
                        :, tile * LANES : (tile + 1) * LANES
                    ]
        for i in range(modes // LANES):
            turned = turn_ref[sub, i].reshape(out_rows, sub_lons, LANES).astype(bf16)
            done_ref[sub, :, :, i * LANES : (i + 1) * LANES] = turned
        copy = pltpu.make_async_copy(
            done_ref.at[sub], out_ref.at[:, pl.ds(sub * sub_lons, sub_lons), :], sems.at[sub]
        )
        copy.start()
        copies.append(copy)
    for copy in copies:
        copy.wait()


def on_device(obs_vals, obs_colat, obs_lon, band_list, counts, w_in, b_in, w_out, b_out):
    bands = lax.axis_size("band")
    levels = lax.axis_size("lev")
    channels = obs_vals.shape[1]
    feats = levels * channels
    modes = LAT_DEV * bands
    sub_lons = LON_DEV // SUBS
    slots = bands * LANES // SUBS
    out_rows = w_out.shape[1]
    vmem = pl.BlockSpec(memory_space=pltpu.VMEM)
    smem = pl.BlockSpec(memory_space=pltpu.SMEM)

    hbm = pl.BlockSpec(memory_space=pltpu.HBM)
    obs = obs_lon.shape[0]
    layers = [w_in, b_in.reshape(1, -1), w_out, b_out.reshape(1, -1)]
    packed, *layers = pl.pallas_call(
        lambda *refs: pack_kernel(bands, levels, *refs),
        out_shape=[pltpu.VMEM((levels * bands, channels, LANES), bf16)]
        + [pltpu.VMEM(layer.shape, layer.dtype) for layer in layers]
        + [pltpu.VMEM((modes, modes), bf16)],
        in_specs=[hbm] * 9,
        out_specs=[vmem] * 6,
        scratch_shapes=[
            pltpu.SMEM((1, bands), jnp.int32),
            pltpu.VMEM((bands, LANES), jnp.int32),
            pltpu.VMEM((obs // LANES, LANES), jnp.int32),
            pltpu.VMEM((obs // LANES, LANES), bf16),
            pltpu.VMEM((channels, obs), bf16),
            pltpu.SemaphoreType.DMA((5,)),
            pltpu.SemaphoreType.DMA((4,)),
        ],
        compiler_params=pltpu.CompilerParams(vmem_limit_bytes=(16 if bands <= 16 else 48) << 20),
        name="pack",
    )(
        counts, band_list[0], obs_lon.reshape(-1, LANES), obs_colat.reshape(-1, LANES), obs_vals[0],
        *layers,
    )

    received = lax.all_to_all(packed, ("lev", "band"), split_axis=0, concat_axis=0, tiled=True)
    received = pltpu.with_memory_space_constraint(received, pltpu.VMEM)
    spread_buffers = SUBS if bands <= 16 else 1
    encoded, overflow = pl.pallas_call(
        lambda *refs: encode_kernel(bands, levels, channels, *refs),
        out_shape=[
            jax.ShapeDtypeStruct((out_rows, LON_DEV, modes), bf16),
            pltpu.SMEM((1,), jnp.int32),
        ],
        in_specs=[vmem] * 6,
        out_specs=[hbm, pl.BlockSpec(memory_space=pltpu.SMEM)],
        scratch_shapes=[
            pltpu.VMEM((spread_buffers, sub_lons * feats, slots), bf16),
            pltpu.VMEM((SUBS, sub_lons * feats, modes), bf16),
            pltpu.VMEM((SUBS, modes // LANES, out_rows * sub_lons, LANES), f32),
            pltpu.VMEM((SUBS, out_rows, sub_lons, modes), bf16),
            pltpu.SemaphoreType.DMA((SUBS,)),
        ],
        compiler_params=pltpu.CompilerParams(vmem_limit_bytes=(24 if bands <= 16 else 56) << 20),
        name="encode",
    )(received, *layers)

    def by_bands():
        vals = whole_copy(obs_vals)
        return whole_copy(by_band(vals, obs_colat, obs_lon, band_list, counts, w_in, b_in, w_out, b_out))

    def again(carry):
        return by_bands(), jnp.zeros_like(carry[1])

    return lax.while_loop(lambda carry: carry[1], again, (encoded, overflow[0] > 0))[0]


def solution(mesh):
    in_specs = (
        P("lev", None, "band"),
        P("band"),
        P("band"),
        P("band", None, None),
        P("band", None),
        P(),
        P(),
        P(None, "lev"),
        P("lev"),
    )
    out_specs = P("lev", "band", None)
    return jax.shard_map(
        on_device, mesh=mesh, in_specs=in_specs, out_specs=out_specs, check_vma=False
    )
```
